32 devices in a mesh: dp: 8 (over z, x), tensor: 4 (over y, core).
Axes of the slice: x: 2, y: 2, z: 4, core: 2. Of those that a mesh axis runs over, the one named last changes fastest.
Arguments:
- frames: bfloat16 [16, 1024, 1024], P('dp', 'tensor'), may hold values from -6 to 6
- lengths: int32 [16], P('dp'), may hold values from 128 to 1024, as said below
- codebook: int32 [16], P('dp'), may hold values from 0 to 6
- ln_gain: float32 [2, 1024], replicated, may hold values from 0.5 to 1.5
- ln_bias: float32 [2, 1024], replicated, may hold values from -1.8 to 1.8
- ada_scale: float32 [7, 2, 1024], replicated, may hold values from 0.25 to 1.75
- ada_shift: float32 [7, 2, 1024], replicated, may hold values from -1.8 to 1.8
- w_qkv: bfloat16 [2, 1024, 3, 1024], P(None, None, None, 'tensor'), may hold values from -0.1875 to 0.1875
- w_out: bfloat16 [2, 1024, 1024], P(None, 'tensor'), may hold values from -0.75 to 0.75
- w_up: bfloat16 [2, 1024, 4096], P(None, None, 'tensor'), may hold values from -0.1875 to 0.1875
- w_down: bfloat16 [2, 4096, 1024], P(None, 'tensor'), may hold values from -0.09375 to 0.09375
- out_grad: bfloat16 [16, 1024, 1024], P('dp', 'tensor'), may hold values from -6 to 6
Outputs:
- hidden_out: bfloat16 [16, 1024, 1024], P('dp', 'tensor')
- frames_grad: float32 [16, 1024, 1024], P('dp', 'tensor')
- grad_ln_gain: float32 [2, 1024], replicated
- grad_ln_bias: float32 [2, 1024], replicated
- grad_ada_scale: float32 [7, 2, 1024], replicated
- grad_ada_shift: float32 [7, 2, 1024], replicated
- grad_w_qkv: float32 [2, 1024, 3, 1024], P(None, None, None, 'tensor')
- grad_w_out: float32 [2, 1024, 1024], P(None, 'tensor')
- grad_w_up: float32 [2, 1024, 4096], P(None, None, 'tensor')
- grad_w_down: float32 [2, 4096, 1024], P(None, 'tensor')
The draws below stay inside these ranges and needn't reach their ends.
Inputs may be any that keep to these rules, and one draw needn't show every extreme that they name: `lengths`: in every run of 2 consecutive utterances that starts at a multiple of 2, one utterance has length 1024.
All inputs are finite; a program needn't handle non-finite values.
Results may differ from the reference program's by a relative error of at most 0.02.
Values may be sent and summed in bfloat16 or wider, within the bound.
A program may use at most 320 MiB of HBM per device.

```python
import jax
import jax.numpy as jnp
from jax import lax

D = 1024
HEADS = 16
FF = 4096
HEAD_DIM = 64
SECTIONS = 7
LEN = 1024
MICRO = 2
SEQS = 16


def draw_lengths(key, part):
    key = jax.random.fold_in(key, 17)
    base_key, slot_key = jax.random.split(key)
    drawn_lengths = jax.random.randint(base_key, (SEQS,), LEN // 8, LEN + 1)
    full_slot = jax.random.randint(slot_key, (SEQS // MICRO,), 0, MICRO)
    slot_of = jnp.arange(SEQS) % MICRO
    groups = jnp.arange(SEQS) // MICRO
    return jnp.where(slot_of == full_slot[groups], LEN, drawn_lengths).astype(jnp.int32)


def drawn_field(key, shape, spread, limit):
    values = jax.random.normal(key, shape, jnp.float32) * spread
    return jnp.clip(values, -limit, limit)


def draw_frames(key, part):
    key = jax.random.fold_in(key, 23)
    return drawn_field(key, (SEQS, LEN, D), 1.0, 6.0).astype(jnp.bfloat16)


def draw_out_grad(key, part):
    key = jax.random.fold_in(key, 29)
    return drawn_field(key, (SEQS, LEN, D), 1.0, 6.0).astype(jnp.bfloat16)


def draw_ln_bias(key, part):
    key = jax.random.fold_in(key, 31)
    return drawn_field(key, (2, D), 0.3, 1.8)


def draw_ada_shift(key, part):
    key = jax.random.fold_in(key, 37)
    return drawn_field(key, (SECTIONS, 2, D), 0.3, 1.8)


def touch_ends(drawn, key, low, top_value):
    place = [jax.random.randint(jax.random.fold_in(key, axis), (), 0, length) for axis, length in enumerate(drawn.shape)]
    widest = drawn.shape.index(max(drawn.shape))
    beside = place[:widest] + [(place[widest] + 1) % drawn.shape[widest]] + place[widest + 1:]
    return drawn.at[tuple(place)].set(low).at[tuple(beside)].set(top_value)


def shard_levels(key, extent, cuts, low, top_value):
    gain, own = 1.0, jax.random.fold_in(key, 6)
    for position, shards_of in cuts:
        heights = jnp.exp(jax.random.uniform(jax.random.fold_in(own, position), (shards_of,), jnp.float32, low / len(cuts), top_value / len(cuts)))
        gain = gain * jnp.repeat(heights, extent[position] // shards_of).reshape([-1 if axis == position else 1 for axis in range(len(extent))])
    return gain


def scatter_about(key, shape, width, most, shards=(), kind=jnp.bfloat16):
    array = width * jax.random.normal(key, shape, jnp.float32)
    if shards:
        array = array * shard_levels(key, shape, shards, -0.22, 0.18)
    return jnp.clip(array, -most, most).astype(kind)


def setup_inputs(seed: int = 0) -> dict:
    seeds = jax.random.split(jax.random.key(seed), 13)
    return {
        "frames": draw_frames(jax.random.fold_in(seeds[12], 71), 0),
        "lengths": draw_lengths(jax.random.fold_in(seeds[12], 71), 0),
        "codebook": touch_ends(jax.random.randint(seeds[2], (SEQS,), 0, SECTIONS), jax.random.fold_in(seeds[2], 1), 0, SECTIONS - 1).astype(jnp.int32),
        "ln_gain": jnp.clip(1.0 + 0.1 * jax.random.normal(seeds[3], (2, D), jnp.float32), 0.5, 1.5),
        "ln_bias": draw_ln_bias(jax.random.fold_in(seeds[12], 71), 0),
        "ada_scale": jnp.clip(1.0 + 0.15 * jax.random.normal(seeds[5], (SECTIONS, 2, D), jnp.float32), 0.25, 1.75),
        "ada_shift": draw_ada_shift(jax.random.fold_in(seeds[12], 71), 0),
        "w_qkv": scatter_about(seeds[7], (2, D, 3, D), D ** -0.5, 0.1875, ((3, 4),)),
        "w_out": scatter_about(seeds[8], (2, D, D), (D // 16) ** -0.5, 0.75, ((1, 4),)),
        "w_up": scatter_about(seeds[9], (2, D, FF), D ** -0.5, 0.1875, ((2, 4),)),
        "w_down": scatter_about(seeds[10], (2, FF, D), FF ** -0.5, 0.09375, ((1, 4),)),
        "out_grad": draw_out_grad(jax.random.fold_in(seeds[12], 71), 0),
    }


@jax.custom_vjp
def low(v):
    return lax.optimization_barrier(v.astype(jnp.bfloat16)).astype(jnp.float32)

@jax.custom_vjp
def low_back(v):
    return v

def low_keep(v):
    return (low(v), None)

def low_pass(kept, grad):
    return (grad,)

def back_keep(v):
    return (v, None)

def back_low(kept, grad):
    return (low(grad),)
low.defvjp(low_keep, low_pass)
low_back.defvjp(back_keep, back_low)

def normalize(states):
    average = lax.optimization_barrier(jnp.mean(states, axis=-1, keepdims=True))
    centred = states - average
    variance = lax.optimization_barrier(jnp.mean(centred * centred, axis=-1, keepdims=True))
    return centred * lax.rsqrt(variance + 1e-05)

def matmul(left, right):
    return jnp.dot(left, right, precision=lax.Precision.HIGHEST)

def attend(queries, keys, values, key_valid, causal):
    scaling = HEAD_DIM ** (-0.5)
    block_rows = min(512, LEN)
    key_pos = jnp.arange(LEN, dtype=jnp.int32)

    def one_block(block_index):
        first_row = block_index * block_rows
        query_rows = lax.dynamic_slice_in_dim(queries, first_row, block_rows, 0)
        scores = jnp.einsum('qhe,khe->hqk', query_rows, keys, precision=lax.Precision.HIGHEST) * scaling
        scores = low_back(scores)
        allowed = key_valid[None, None, :]
        if causal:
            query_pos = first_row + jnp.arange(block_rows, dtype=jnp.int32)
            allowed = allowed & (key_pos[None, None, :] <= query_pos[None, :, None])
        scores = jnp.where(allowed, scores, -1e+30)
        weights = low(jax.nn.softmax(scores, axis=-1))
        return jnp.einsum('hqk,khe->qhe', weights, values, precision=lax.Precision.HIGHEST)
    blocks = lax.map(jax.checkpoint(one_block), jnp.arange(LEN // block_rows, dtype=jnp.int32))
    return blocks.reshape(LEN, HEADS * HEAD_DIM)

def run_layer(states, gains, shifts, qkv_weight, out_weight, up_weight, down_weight, key_valid, causal):
    entering = low(normalize(states) * gains[0] + shifts[0])
    projected = low_back(low(matmul(entering, qkv_weight.reshape(D, 3 * D))))
    projected = projected.reshape(LEN, 3, HEADS, HEAD_DIM)
    attended = low_back(low(attend(projected[:, 0], projected[:, 1], projected[:, 2], key_valid, causal)))
    middle = states + low_back(matmul(attended, out_weight))
    entering = low(normalize(middle) * gains[1] + shifts[1])
    hidden = low_back(matmul(entering, up_weight))
    active = low(jax.nn.gelu(hidden, approximate=False))
    return middle + low_back(matmul(active, down_weight))

def forward(states, params, key_valid, section_index):
    ln_gain, ln_bias, ada_scale, ada_shift, w_qkv, w_out, w_up, w_down = params
    states = run_layer(states, ln_gain, ln_bias, w_qkv[0], w_out[0], w_up[0], w_down[0], key_valid, True)
    return run_layer(states, ada_scale[section_index], ada_shift[section_index], w_qkv[1], w_out[1], w_up[1], w_down[1], key_valid, False)

def reference(frames, lengths, codebook, ln_gain, ln_bias, ada_scale, ada_shift, w_qkv, w_out, w_up, w_down, out_grad):
    params = tuple((weight.astype(jnp.float32) for weight in (ln_gain, ln_bias, ada_scale, ada_shift, w_qkv, w_out, w_up, w_down)))
    key_pos = jnp.arange(LEN, dtype=jnp.int32)

    def scan_step(totals, scan_item):
        frame_rows, length, section_index, cotangent = scan_item
        key_valid = key_pos < length

        def run_layers(inputs, weights):
            return forward(inputs, weights, key_valid, section_index)
        outputs, pullback = jax.vjp(run_layers, frame_rows.astype(jnp.float32), params)
        input_grads, weight_grads = pullback(cotangent.astype(jnp.float32))
        totals = jax.tree.map(jnp.add, totals, weight_grads)
        return (totals, (outputs.astype(jnp.bfloat16), input_grads))
    zero_grads = tuple((jnp.zeros_like(weight) for weight in params))
    totals, (hidden_out, frames_grad) = lax.scan(scan_step, zero_grads, (frames, lengths, codebook, out_grad))
    return (hidden_out, frames_grad, totals[0], totals[1], totals[2], totals[3], totals[4], totals[5], totals[6], totals[7])
```

```python
import jax
import jax.numpy as jnp
from jax import lax
from jax.sharding import PartitionSpec as P

HEAD_DIM = 64
BF = jnp.bfloat16
F32 = jnp.float32


def swap_tensor(x, bit):
    pairs = [(i, i ^ bit) for i in range(lax.axis_size("tensor"))]
    return lax.ppermute(x, "tensor", pairs)


def swap_dp(x, bit):
    pairs = [(i, i ^ bit) for i in range(lax.axis_size("dp"))]
    return lax.ppermute(x, "dp", pairs)


def in_order(flag, mine, theirs):
    return jnp.where(
        flag == 0, jnp.concatenate([mine, theirs], 0), jnp.concatenate([theirs, mine], 0)
    )


def normalize(states):
    average = jnp.mean(states, axis=-1, keepdims=True)
    centred = states - average
    variance = jnp.mean(centred * centred, axis=-1, keepdims=True)
    inverse = lax.rsqrt(variance + 1e-05)
    return (centred * inverse, inverse)


def norm_backward(normed, inverse, grad_normed):
    mean_grad = jnp.mean(grad_normed, axis=-1, keepdims=True)
    mean_proj = jnp.mean(grad_normed * normed, axis=-1, keepdims=True)
    return inverse * (grad_normed - mean_grad - normed * mean_proj)


def gelu_slope(hidden):
    normal_cdf = 0.5 * (1.0 + jax.scipy.special.erf(hidden * 0.7071067811865476))
    density = jnp.exp(-0.5 * hidden * hidden) * 0.3989422804014327
    return normal_cdf + hidden * density


def mm(left, right):
    return jnp.dot(left, right, preferred_element_type=F32)


def mm_rows(left, right):
    return lax.dot_general(left, right, (((0,), (0,)), ((), ())), preferred_element_type=F32)


def mm_cols(left, right):
    return lax.dot_general(left, right, (((1,), (1,)), ((), ())), preferred_element_type=F32)


def gather_core(mine):
    return jnp.concatenate([mine, swap_tensor(mine, 1)], axis=0)


def scatter_core(partial):
    half = partial.shape[0] // 2
    return partial[:half] + swap_tensor(partial[half:].astype(BF), 1).astype(F32)


def fetch_foreign(weight):
    dp = lax.axis_index("dp")
    rows = weight.shape[0]
    if lax.axis_size("dp") % 4 or rows % 64:
        return swap_tensor(weight, 2)
    quarter = rows // 4
    piece = lax.dynamic_slice_in_dim(weight, lax.rem(dp, 4) * quarter, quarter, 0)
    piece = swap_tensor(piece, 2)
    bit0 = lax.rem(dp, 2)
    bit1 = lax.rem(dp // 2, 2)
    pair = in_order(bit0, piece, swap_dp(piece, 1))
    return in_order(bit1, pair, swap_dp(pair, 2))


def reduce_dp(grad):
    dp = lax.axis_index("dp")
    bits = []
    size = lax.axis_size("dp")
    bit = 1
    while bit < size:
        bits.append(bit)
        bit *= 2
    value = grad.astype(BF)
    for bit in bits:
        half = value.shape[0] // 2
        flag = lax.rem(dp // bit, 2)
        send = lax.dynamic_slice_in_dim(value, (1 - flag) * half, half, 0)
        keep = lax.dynamic_slice_in_dim(value, flag * half, half, 0)
        value = (keep.astype(F32) + swap_dp(send, bit).astype(F32)).astype(BF)
    for bit in reversed(bits):
        flag = lax.rem(dp // bit, 2)
        value = in_order(flag, value, swap_dp(value, bit))
    return value.astype(F32)


def finish_grad(own, foreign):
    back = swap_tensor(foreign.astype(BF), 2)
    return reduce_dp(own + back.astype(F32))


def masked_scores(query_rows, keys, query_pos, key_pos, key_valid, causal, scaling):
    scores = (
        jnp.einsum("qhe,khe->hqk", query_rows, keys, preferred_element_type=F32) * scaling
    )
    allowed = key_valid[None, None, :]
    if causal:
        allowed = allowed & (key_pos[None, None, :] <= query_pos[None, :, None])
    return jnp.where(allowed, scores, -1e30)


def attention_forward(queries, keys, values, pos, key_valid, causal, scaling):
    length = queries.shape[0]
    block_rows = length // 2
    outputs = []
    logsums = []
    for first_row in range(0, length, block_rows):
        rows = slice(first_row, first_row + block_rows)
        scores = masked_scores(queries[rows], keys, pos[rows], pos, key_valid, causal, scaling)
        row_max = jnp.max(scores, axis=-1, keepdims=True)
        logsum = row_max + jnp.log(jnp.sum(jnp.exp(scores - row_max), axis=-1, keepdims=True))
        weights = jnp.exp(scores - logsum).astype(BF)
        mixed_rows = jnp.einsum("hqk,khe->qhe", weights, values, preferred_element_type=F32)
        outputs.append(mixed_rows.reshape(block_rows, -1).astype(BF))
        logsums.append(logsum[:, :, 0])
    return (jnp.concatenate(outputs, axis=0), jnp.concatenate(logsums, axis=1))


def attention_backward(queries, keys, values, logsums, grad_mixed, pos, key_valid, causal, scaling):
    length = queries.shape[0]
    block_rows = length // 2
    grad_heads = grad_mixed.reshape(queries.shape)
    grad_keys = jnp.zeros(keys.shape, F32)
    grad_values = jnp.zeros(values.shape, F32)
    query_grads = []
    for first_row in range(0, length, block_rows):
        rows = slice(first_row, first_row + block_rows)
        query_rows = queries[rows]
        grad_rows = grad_heads[rows]
        scores = masked_scores(query_rows, keys, pos[rows], pos, key_valid, causal, scaling)
        row_probs = jnp.exp(scores - logsums[:, rows, None])
        grad_probs = jnp.einsum("qhe,khe->hqk", grad_rows, values, preferred_element_type=F32)
        grad_values = grad_values + jnp.einsum(
            "hqk,qhe->khe", row_probs.astype(BF), grad_rows, preferred_element_type=F32
        )
        grad_scores = row_probs * (
            grad_probs - jnp.sum(row_probs * grad_probs, axis=-1, keepdims=True)
        )
        grad_scores = grad_scores.astype(BF)
        query_grads.append(
            jnp.einsum("hqk,khe->qhe", grad_scores, keys, preferred_element_type=F32) * scaling
        )
        grad_keys = (
            grad_keys
            + jnp.einsum("hqk,qhe->khe", grad_scores, query_rows, preferred_element_type=F32)
            * scaling
        )
    grad_queries = jnp.concatenate(query_grads, axis=0)
    stacked = jnp.stack([grad_queries, grad_keys, grad_values], axis=1).astype(BF)
    return stacked.reshape(length, -1)


def layer_forward(states, gains, shifts, weights, pos, key_valid, causal, scaling):
    normed_att, inverse_att = normalize(states)
    gathered_att = gather_core((normed_att * gains[0] + shifts[0]).astype(BF))
    length = gathered_att.shape[0]
    heads = []
    for part in range(2):
        projected = mm(gathered_att, weights["qkv"][part]).astype(BF)
        split = projected.reshape(length, 3, -1, HEAD_DIM)
        attended, logsums = attention_forward(
            split[:, 0], split[:, 1], split[:, 2], pos, key_valid, causal, scaling
        )
        heads.append((split, attended, logsums))
    middle = states + scatter_core(
        mm(heads[0][1], weights["out"][0]) + mm(heads[1][1], weights["out"][1])
    )
    normed_ffn, inverse_ffn = normalize(middle)
    gathered_ffn = gather_core((normed_ffn * gains[1] + shifts[1]).astype(BF))
    units = []
    for part in range(2):
        hidden = mm(gathered_ffn, weights["up"][part])
        active = jax.nn.gelu(hidden, approximate=False).astype(BF)
        units.append((hidden, active))
    result = middle + scatter_core(
        mm(units[0][1], weights["down"][0]) + mm(units[1][1], weights["down"][1])
    )
    kept = (normed_att, inverse_att, gathered_att, heads, normed_ffn, inverse_ffn, gathered_ffn, units)
    return result, kept


def layer_backward(grad_states, kept, gains, weights, pos, key_valid, causal, scaling):
    (normed_att, inverse_att, gathered_att, heads, normed_ffn, inverse_ffn, gathered_ffn, units) = kept
    grads = {"qkv": [], "out": [], "up": [], "down": []}
    gathered_grad = gather_core(grad_states.astype(BF))
    partial = 0.0
    for part in range(2):
        hidden, active = units[part]
        grad_active = mm_cols(gathered_grad, weights["down"][part])
        grad_hidden = (grad_active * gelu_slope(hidden)).astype(BF)
        grads["down"].append(mm_rows(active, gathered_grad))
        grads["up"].append(mm_rows(gathered_ffn, grad_hidden))
        partial = partial + mm_cols(grad_hidden, weights["up"][part])
    grad_entering = scatter_core(partial)
    gain_ffn = jnp.sum(grad_entering * normed_ffn, axis=0)
    shift_ffn = jnp.sum(grad_entering, axis=0)
    grad_middle = grad_states + norm_backward(normed_ffn, inverse_ffn, grad_entering * gains[1])
    gathered_grad = gather_core(grad_middle.astype(BF))
    partial = 0.0
    for part in range(2):
        split, attended, logsums = heads[part]
        grad_attended = mm_cols(gathered_grad, weights["out"][part]).astype(BF)
        grads["out"].append(mm_rows(attended, gathered_grad))
        grad_projected = attention_backward(
            split[:, 0], split[:, 1], split[:, 2], logsums, grad_attended, pos, key_valid, causal, scaling
        )
        grads["qkv"].append(mm_rows(gathered_att, grad_projected))
        partial = partial + mm_cols(grad_projected, weights["qkv"][part])
    grad_entering = scatter_core(partial)
    gain_att = jnp.sum(grad_entering * normed_att, axis=0)
    shift_att = jnp.sum(grad_entering, axis=0)
    grad_input = grad_middle + norm_backward(normed_att, inverse_att, grad_entering * gains[0])
    return (
        grad_input,
        {name: finish_grad(*pair) for name, pair in grads.items()},
        jnp.stack([gain_att, gain_ffn]),
        jnp.stack([shift_att, shift_ffn]),
    )


def per_device(
    frames, lengths, codebook, ln_gain, ln_bias, ada_scale, ada_shift, w_qkv, w_out, w_up, w_down, out_grad
):
    tensor = lax.axis_index("tensor")
    chip = tensor // 2
    core = lax.rem(tensor, 2)
    block = frames.shape[1]
    length = block * lax.axis_size("tensor")
    scaling = HEAD_DIM ** (-0.5)

    def pick(pair):
        return jnp.where(chip == 0, pair[0], pair[1])

    def other(pair):
        return jnp.where(chip == 0, pair[1], pair[0])

    def take_rows(array):
        return in_order(chip, pick(array), swap_tensor(other(array), 2)).astype(F32)

    blocks = [core, 2 + core, 1 - core, 3 - core]
    pos = jnp.concatenate([index * block + jnp.arange(block) for index in blocks])
    key_valid = pos < pick(lengths)
    section = pick(codebook)
    section_match = (jnp.arange(ada_scale.shape[0]) == section)[:, None, None]
    gains = (ln_gain, jnp.sum(jnp.where(section_match, ada_scale, 0.0), axis=0))
    shifts = (ln_bias, jnp.sum(jnp.where(section_match, ada_shift, 0.0), axis=0))
    weights = []
    for layer in range(2):
        own = {
            "qkv": w_qkv[layer].reshape(w_qkv.shape[1], -1),
            "out": w_out[layer],
            "up": w_up[layer],
            "down": w_down[layer],
        }
        weights.append({name: (own[name], fetch_foreign(own[name])) for name in own})
    states = take_rows(frames)
    kept = [None, None]
    for layer in range(2):
        states, kept[layer] = layer_forward(
            states, gains[layer], shifts[layer], weights[layer], pos, key_valid, layer == 0, scaling
        )

    def give_rows(array):
        first, second = array[:block], array[block:]
        mine = jnp.where(chip == 0, first, second)
        theirs = swap_tensor(jnp.where(chip == 0, second, first), 2)
        return in_order(chip, mine[None], theirs[None])

    hidden_out = give_rows(states.astype(BF))
    grad_states = take_rows(out_grad)
    sums = [None, None]
    gain_grads = [None, None]
    shift_grads = [None, None]
    for layer in (1, 0):
        grad_states, sums[layer], gain_grads[layer], shift_grads[layer] = layer_backward(
            grad_states, kept[layer], gains[layer], weights[layer], pos, key_valid, layer == 0, scaling
        )
    frames_grad = give_rows(grad_states.astype(BF)).astype(F32)
    sections = ada_scale.shape[0]
    small = jnp.concatenate(
        [
            gain_grads[0],
            shift_grads[0],
            jnp.where(section_match, gain_grads[1][None], 0.0).reshape(2 * sections, -1),
            jnp.where(section_match, shift_grads[1][None], 0.0).reshape(2 * sections, -1),
        ]
    )
    small = lax.psum(small, ("dp", "tensor"))

    def both(name, shape):
        return jnp.stack([sums[layer][name].reshape(shape[1:]) for layer in range(2)])

    return (
        hidden_out,
        frames_grad,
        small[0:2],
        small[2:4],
        small[4 : 4 + 2 * sections].reshape(ada_scale.shape),
        small[4 + 2 * sections :].reshape(ada_scale.shape),
        both("qkv", w_qkv.shape),
        both("out", w_out.shape),
        both("up", w_up.shape),
        both("down", w_down.shape),
    )


def solution(mesh):
    placed = (
        P("dp", "tensor", None),
        P("dp"),
        P("dp"),
        P(),
        P(),
        P(),
        P(),
        P(None, None, None, "tensor"),
        P(None, "tensor", None),
        P(None, None, "tensor"),
        P(None, "tensor", None),
        P("dp", "tensor", None),
    )
    return jax.shard_map(
        per_device,
        mesh=mesh,
        in_specs=placed,
        out_specs=(
            P("dp", "tensor", None),
            P("dp", "tensor", None),
            P(),
            P(),
            P(),
            P(),
            P(None, None, None, "tensor"),
            P(None, "tensor", None),
            P(None, None, "tensor"),
            P(None, "tensor", None),
        ),
        check_vma=False,
    )
```

```python
import functools
from typing import Any, NamedTuple

import jax
import jax.numpy as jnp
from jax import lax
from jax.experimental import pallas as pl
from jax.experimental.pallas import tpu as pltpu
from jax.sharding import PartitionSpec as P

HEAD_DIM = 64
BF = jnp.bfloat16
F32 = jnp.float32
HIGH = lax.Precision.HIGHEST
MESH = pl.DeviceIdType.MESH
VMEM_BYTES = 60 << 20
LANES = 128


def mm(left, right):
    return jnp.dot(left, right, preferred_element_type=F32)


def mm_rows(left, right):
    return lax.dot_general(left, right, (((0,), (0,)), ((), ())), preferred_element_type=F32)


def mm_cols(left, right, precision=None):
    return lax.dot_general(
        left, right, (((1,), (1,)), ((), ())), precision=precision, preferred_element_type=F32
    )


def head_of_lane(shape):
    return lax.broadcasted_iota(jnp.int32, shape, len(shape) - 1) // HEAD_DIM


def at(start, size, unit):
    return pl.ds(pl.multiple_of(start, unit), size)


def flip(index, bit):
    return index + bit - 2 * bit * lax.rem(index // bit, 2)


def dp_bits(size):
    bits = []
    while 2 ** len(bits) < size:
        bits.append(2 ** len(bits))
    return bits


def attend_part(causal, n_ref, w_ref, bias_ref, qkva_ref, lse_ref):
    length = n_ref.shape[0]
    part = qkva_ref.shape[1] // 4
    block = length // 4
    scaling = HEAD_DIM ** (-0.5)

    def project(index, _):
        rows = at(index * block, block, block)
        qkva_ref[rows, : 3 * part] = mm(n_ref[rows, :], w_ref[:, : 3 * part]).astype(BF)
        return 0

    lax.fori_loop(0, 4, project, 0)

    def pair_body(pair, _):
        q_cols, k_cols, v_cols, a_cols = [at(i * part + pair * LANES, LANES, LANES) for i in range(4)]
        for first in range(0, length, block):
            rows = pl.ds(first, block)
            reach = first + block if causal else length
            queries = qkva_ref[rows, q_cols] * jnp.asarray(scaling, BF)
            keys = qkva_ref[pl.ds(0, reach), k_cols]
            values = qkva_ref[pl.ds(0, reach), v_cols]
            bias = bias_ref[:, pl.ds(0, reach)]
            head = head_of_lane(queries.shape)
            lanes = lax.broadcasted_iota(jnp.int32, (block, LANES), 1)
            mixed = None
            stats = jnp.zeros((block, LANES), F32)
            for which in range(2):
                scores = mm_cols(jnp.where(head == which, queries, jnp.zeros_like(queries)), keys) + bias
                if causal:
                    query_at = first + lax.broadcasted_iota(jnp.int32, scores.shape, 0)
                    key_at = lax.broadcasted_iota(jnp.int32, scores.shape, 1)
                    scores = jnp.where(key_at <= query_at, scores, -1e30)
                row_max = jnp.max(scores, axis=-1, keepdims=True)
                raised = jnp.exp(scores - row_max)
                total = jnp.sum(raised, axis=-1, keepdims=True)
                one = mm(raised.astype(BF), values) * (1.0 / total)
                mixed = one if mixed is None else jnp.where(head == 0, mixed, one)
                stats = jnp.where(lanes == which, row_max + jnp.log(total), stats)
            qkva_ref[rows, a_cols] = mixed.astype(BF)
            square = lax.broadcasted_iota(jnp.int32, (8, LANES), 1)
            pick = (square == lax.broadcasted_iota(jnp.int32, (8, LANES), 0)).astype(F32)
            lse_ref[pair, :, rows] = mm_cols(pick, stats, HIGH)
        return 0

    lax.fori_loop(0, part // LANES, pair_body, 0)


def attend_part_back(causal, grad_att_ref, qkva_ref, lse_of, bias_ref, dqkv_ref, dk_ref, dv_ref):
    length = qkva_ref.shape[0]
    part = qkva_ref.shape[1] // 4
    block = length // 4
    scaling = HEAD_DIM ** (-0.5)

    def pair_body(pair, _):
        q_cols, k_cols, v_cols, a_cols = [at(i * part + pair * LANES, LANES, LANES) for i in range(4)]
        g_cols = at(pair * LANES, LANES, LANES)
        dk_ref[...] = jnp.zeros_like(dk_ref)
        dv_ref[...] = jnp.zeros_like(dv_ref)
        keys_turned = qkva_ref[:, k_cols].astype(F32).T.astype(BF)
        feature = lax.broadcasted_iota(jnp.int32, keys_turned.shape, 0) // HEAD_DIM
        turned = [
            jnp.where(feature == which, keys_turned, jnp.zeros_like(keys_turned)) for which in range(2)
        ]
        for first in range(0, length, block):
            rows = pl.ds(first, block)
            reach = first + block if causal else length
            queries = qkva_ref[rows, q_cols] * jnp.asarray(scaling, BF)
            grads = grad_att_ref[rows, g_cols]
            head = head_of_lane(queries.shape)
            pick = (head_of_lane((8, LANES)) == lax.broadcasted_iota(jnp.int32, (8, LANES), 0)).astype(F32)
            product = grads.astype(F32) * qkva_ref[rows, a_cols].astype(F32)
            delta = mm_cols(pick, product, HIGH)
            lse = lse_of(pair, rows)
            keys = qkva_ref[pl.ds(0, reach), k_cols]
            values = qkva_ref[pl.ds(0, reach), v_cols]
            bias = bias_ref[pl.ds(0, reach), :]
            dq_turned = None
            for which in range(2):
                queries_one = jnp.where(head == which, queries, jnp.zeros_like(queries))
                grads_one = jnp.where(head == which, grads, jnp.zeros_like(grads))
                scores = mm_cols(keys, queries_one) + bias
                if causal:
                    key_at = lax.broadcasted_iota(jnp.int32, scores.shape, 0)
                    query_at = first + lax.broadcasted_iota(jnp.int32, scores.shape, 1)
                    scores = jnp.where(key_at <= query_at, scores, -1e30)
                probs = jnp.exp(scores - lse[which : which + 1])
                grad_probs = mm_cols(values, grads_one)
                grad_scores = (probs * (grad_probs - delta[which : which + 1])).astype(BF)
                dv_ref[pl.ds(0, reach), :] += mm(probs.astype(BF), grads_one)
                dk_ref[pl.ds(0, reach), :] += mm(grad_scores, queries_one)
                one = mm(turned[which][:, :reach], grad_scores)
                dq_turned = one if dq_turned is None else dq_turned + one
            dqkv_ref[rows, q_cols] = (dq_turned.T * scaling).astype(BF)
        dqkv_ref[:, k_cols] = dk_ref[...].astype(BF)
        dqkv_ref[:, v_cols] = dv_ref[...].astype(BF)
        return 0

    lax.fori_loop(0, part // LANES, pair_body, 0)


def gelu_parts(hidden):
    bell = jnp.exp(-0.5 * hidden * hidden)
    t = 1.0 / (1.0 + 0.23164189 * jnp.abs(hidden))
    poly = 0.5307027145
    poly = poly * t - 0.7265760135
    poly = poly * t + 0.7107068705
    poly = poly * t - 0.142248368
    poly = poly * t + 0.127414796
    tail = poly * t * bell
    cdf = jnp.where(hidden >= 0, 1.0 - tail, tail)
    return hidden * cdf, cdf + hidden * bell * 0.3989422804014327


class Slots:
    def __init__(self, buffers, sems):
        self.buffers = buffers
        self.sems = sems
        self.free = list(range(buffers.shape[0]))
        self.held = {}

    def load(self, name, source):
        slot = self.free.pop(0)
        copy = pltpu.make_async_copy(source, self.buffers.at[slot], self.sems.at[slot])
        copy.start()
        self.held[name] = [slot, copy]

    def get(self, name):
        slot, copy = self.held[name]
        if copy is not None:
            copy.wait()
            self.held[name][1] = None
        return self.buffers.at[slot]

    def drop(self, *names):
        for name in names:
            self.free.append(self.held.pop(name)[0])


class Summing:
    AHEAD = 4

    def __init__(self, bits, own, foreign, landed, out, acc, seg, y_view, own_view, rbufs, send_sem, recv_sem, copy_sem, view_sem):
        self.bits, self.own, self.foreign, self.landed, self.out = bits, own, foreign, landed, out
        self.acc, self.seg, self.y_view, self.own_view, self.rbufs = acc, seg, y_view, own_view, rbufs
        self.send_sem, self.recv_sem, self.copy_sem, self.view_sem = send_sem, recv_sem, copy_sem, view_sem
        self.chunks, self.rows, self.columns = own.shape
        self.ring = acc.shape[0]
        self.stages = 2 * len(bits) + 1
        self.dp = lax.axis_index("dp")
        self.tensor = lax.axis_index("tensor")
        self.step = 0
        self.started = 0
        self.ready = 0
        row, column = 0, 0
        self.sizes, self.keep, self.send = [], [], []
        for half_rows, half_columns, bit, by_rows in halvings(bits, self.rows, self.columns):
            flag = lax.rem(self.dp // bit, 2)
            if by_rows:
                keep = (row + flag * half_rows, column)
                send = (row + (1 - flag) * half_rows, column)
            else:
                keep = (row, column + flag * half_columns)
                send = (row, column + (1 - flag) * half_columns)
            row, column = keep
            self.sizes.append((half_rows, half_columns))
            self.keep.append(keep)
            self.send.append(send)

    def region(self, where, size):
        return at(where[0], size[0], 16), at(where[1], size[1], LANES)

    def copy(self, s, c):
        count = len(self.bits)
        if s == 0:
            source, target = self.foreign.at[c], self.landed.at[c]
            device = {"tensor": flip(self.tensor, 2)}
        elif s <= count:
            i = s - 1
            rows, columns = self.region(self.send[i], self.sizes[i])
            source = self.acc.at[c % self.ring, rows, columns]
            target = self.rbufs[i].at[c % self.ring]
            device = {"dp": flip(self.dp, self.bits[i])}
        else:
            i = 2 * count - s
            rows, columns = self.region(self.keep[i], self.sizes[i])
            target = self.out.at[c, rows, columns]
            source = self.seg.at[c] if i == count - 1 else target
            device = {"dp": flip(self.dp, self.bits[i])}
        return pltpu.make_async_remote_copy(
            src_ref=source,
            dst_ref=target,
            send_sem=self.send_sem.at[s, c],
            recv_sem=self.recv_sem.at[s, c],
            device_id=device,
            device_id_type=MESH,
        )

    def seg_copy(self, c):
        rows, columns = self.region(self.keep[-1], self.sizes[-1])
        return pltpu.make_async_copy(self.seg.at[c], self.out.at[c, rows, columns], self.copy_sem.at[c])

    def views(self, c):
        return (
            pltpu.make_async_copy(self.landed.at[c], self.y_view, self.view_sem.at[0]),
            pltpu.make_async_copy(self.own.at[c], self.own_view, self.view_sem.at[1]),
        )

    def finish(self, s, c):
        count = len(self.bits)
        slot = c % self.ring
        if s == 0:
            for view in self.views(c):
                view.wait()
            if c >= self.ring:
                for stage in range(1, count + 1):
                    self.copy(stage, c - self.ring).wait_send()
            self.acc[slot] = (self.own_view[...].astype(F32) + self.y_view[...].astype(F32)).astype(BF)
            return
        self.copy(s, c).wait_recv()
        if s <= count:
            i = s - 1
            rows, columns = self.region(self.keep[i], self.sizes[i])
            total = self.acc[slot, rows, columns].astype(F32) + self.rbufs[i][slot].astype(F32)
            if s == count:
                self.seg[c] = total.astype(BF)
                self.seg_copy(c).start()
            else:
                self.acc[slot, rows, columns] = total.astype(BF)
        elif s == count + 1:
            self.seg_copy(c).wait()

    def advance(self):
        first = self.step
        if first < self.chunks:
            self.copy(0, first).wait_recv()
            for view in self.views(first):
                view.start()
        for s in range(self.stages, 0, -1):
            c = first + 1 - s
            if 0 <= c < self.chunks:
                self.finish(s - 1, c)
                if s < self.stages:
                    self.copy(s, c).start()
        self.step += 1
        self.feed()

    def feed(self):
        while self.started < min(self.ready, self.step + self.AHEAD):
            self.copy(0, self.started).start()
            self.started += 1

    def drain(self):
        while self.step < self.chunks + self.stages - 1:
            self.advance()
        count = len(self.bits)
        for c in range(self.chunks):
            for s in range(self.stages):
                if not (1 <= s <= count and c + self.ring < self.chunks):
                    self.copy(s, c).wait_send()


def halvings(bits, rows, columns):
    steps = []
    for bit in bits:
        by_rows = rows >= 32
        rows, columns = (rows // 2, columns) if by_rows else (rows, columns // 2)
        steps.append((rows, columns, bit, by_rows))
    return steps


def back_kernel(bits, *refs):
    r, refs = BackIn(*refs[: len(BackIn._fields)]), refs[len(BackIn._fields) :]
    o, refs = BackOut(*refs[: len(BackOut._fields)]), refs[len(BackOut._fields) :]
    b, rbufs = BackScratch(*refs[: len(BackScratch._fields)]), refs[len(BackScratch._fields) :]
    dp = lax.axis_index("dp")
    tensor = lax.axis_index("tensor")
    chip = tensor // 2
    core = lax.rem(tensor, 2)
    half, width = b.state.shape
    length = 2 * half
    block = length // 4
    core_partner = {"tensor": flip(tensor, 1)}
    partners = [core_partner, {"tensor": flip(tensor, 2)}] + [{"dp": flip(dp, bit)} for bit in bits]

    barrier = pltpu.get_barrier_semaphore()
    for partner in partners:
        pl.semaphore_signal(barrier, inc=1, device_id=partner, device_id_type=MESH)
    pl.semaphore_wait(barrier, len(partners))

    slots = Slots(b.slots, b.slot_sem)
    summing = Summing(
        bits, o.own, o.foreign, o.landed, o.total, b.acc, b.seg, b.y_view, b.own_view,
        rbufs, b.send_sem, b.recv_sem, b.copy_sem, b.view_sem,
    )
    per_matrix = length // summing.rows
    vec = b.vec
    vec[...] = jnp.zeros_like(vec)

    def remote(source, target, sem, device):
        return pltpu.make_async_remote_copy(
            src_ref=source,
            dst_ref=target,
            send_sem=b.ex_send.at[sem],
            recv_sem=b.ex_recv.at[sem],
            device_id=device,
            device_id_type=MESH,
        )

    def exchange_copies(turn):
        full = b.full.at[turn % 2]
        spans = [at((2 * j + core) * block, block, block) for j in range(2)]
        return [remote(full.at[s], full.at[s], 4 * turn + j, core_partner) for j, s in enumerate(spans)]

    def exchange_start(turn, j):
        exchange_copies(turn)[j].start()

    def exchange_wait(turn):
        for copy in exchange_copies(turn):
            copy.wait()

    def scatter_copies(turn):
        return [
            remote(
                b.rs_send.at[pl.ds(j * block, block)],
                b.rs_recv.at[turn % 2, pl.ds(j * block, block)],
                4 * turn + 2 + j,
                core_partner,
            )
            for j in range(2)
        ]

    def scatter(turn, partial):
        copies = scatter_copies(turn)
        for j in range(2):
            span = at((2 * j + 1 - core) * block, block, block)
            b.rs_send[pl.ds(j * block, block), :] = partial(span).astype(BF)
            copies[j].start()
        for j in range(2):
            span = at((2 * j + core) * block, block, block)
            b.keep[pl.ds(j * block, block), :] = partial(span)
        for copy in copies:
            copy.wait()

    def norm_back(turn, layer, which, normed_copy, inverse_copy, last):
        normed_copy.wait()
        inverse_copy.wait()
        index = 4 * layer + 2 * which
        gain = r.gains[2 * layer + which : 2 * layer + which + 1, :]
        step = 128

        def rows_body(i, _):
            span = at(i * step, step, step)
            grad = b.keep[span, :] + b.rs_recv[turn % 2, span, :].astype(F32)
            normed = b.normed[span, :]
            moved = grad * gain
            mean_grad = jnp.mean(moved, axis=-1, keepdims=True)
            mean_proj = jnp.mean(moved * normed, axis=-1, keepdims=True)
            state = b.state[span, :] + b.inverse[span, :1] * (moved - mean_grad - normed * mean_proj)
            b.state[span, :] = state
            vec[index : index + 1, :] += jnp.sum(grad * normed, axis=0, keepdims=True)
            vec[index + 1 : index + 2, :] += jnp.sum(grad, axis=0, keepdims=True)
            return 0

        lax.fori_loop(0, half // step, rows_body, 0)

    def gather(turn):
        for j in range(2):
            span = at((2 * j + core) * block, block, block)
            b.full[turn % 2, span, :] = b.state[pl.ds(j * block, block), :].astype(BF)
            exchange_start(turn, j)

    def store_chunks(where, matrix, chunk_of, previous):
        if previous is not None:
            previous.wait()
        stage = b.stage

        def body(i, _):
            chunk_of(i, at(i * summing.rows, summing.rows, summing.rows))
            return 0

        lax.fori_loop(0, per_matrix, body, 0)
        copy = pltpu.make_async_copy(
            stage, where.at[pl.ds(matrix * per_matrix, per_matrix)], b.stage_sem.at[0]
        )
        copy.start()
        return copy

    def into_stage(i, value, columns=slice(None)):
        b.stage[i, :, columns] = value.astype(BF)

    state_copy = pltpu.make_async_copy(r.grad_in, b.state, b.misc_sem.at[0])
    state_copy.start()
    slots.load((DOWN, 1), r.foreign_weights.at[1, 2])
    slots.load((SLOPE, 1), r.mats.at[1, 7])
    slots.load((ACT, 1), r.mats.at[1, 5])
    slots.load(ROWS, r.mats.at[1, 3])
    state_copy.wait()
    gather(0)
    pending = None

    for layer in (1, 0):
        base = 0 if layer == 1 else 3
        turn = 0 if layer == 1 else 2
        exchange_wait(turn)
        full = b.full.at[turn % 2]
        normed_copy = pltpu.make_async_copy(r.norms.at[layer, 1], b.normed, b.misc_sem.at[1])
        normed_copy.start()
        inverse_copy = pltpu.make_async_copy(r.inverses.at[layer, 1], b.inverse, b.misc_sem.at[2])
        inverse_copy.start()
        for part in (1, 0):
            down, slope = slots.get((DOWN, part)), slots.get((SLOPE, part))
            dpre = b.dpre.at[part]

            def slope_body(i, _, down=down, slope=slope, dpre=dpre):
                rows = at(i * 256, 256, 256)
                dpre[rows, :] = (mm_cols(full[rows, :], down[...]) * slope[rows, :].astype(F32)).astype(BF)
                return 0

            lax.fori_loop(0, length // 256, slope_body, 0)
            slots.drop((DOWN, part), (SLOPE, part))
            if part == 1:
                slots.load((DOWN, 0), r.w_down.at[layer])
                slots.load((SLOPE, 0), r.mats.at[layer, 6])
            else:
                slots.load((UP, 0), r.w_up.at[layer])
            act, n_full = slots.get((ACT, part)), slots.get(ROWS)
            where = o.foreign if part == 1 else o.own

            def down_chunk(i, rows, act=act):
                into_stage(i, mm_rows(act[:, rows], full[...]))

            def up_chunk(i, rows, n_full=n_full, dpre=dpre):
                into_stage(i, mm_rows(n_full[:, rows], dpre[...]))

            pending = store_chunks(where, base, down_chunk, pending)
            slots.drop((ACT, part))
            if part == 1:
                slots.load((ACT, 0), r.mats.at[layer, 4])
            else:
                slots.load((UP, 1), r.foreign_weights.at[layer, 1])
            pending = store_chunks(where, base + 1, up_chunk, pending)
            if part == 1:
                pending.wait()
                pending = None
                summing.ready = (base + 2) * per_matrix
                summing.feed()
            if layer == 0:
                summing.advance()
        slots.drop(ROWS)
        pending.wait()
        pending = None
        summing.advance()
        ups = [slots.get((UP, 0)), slots.get((UP, 1))]

        def up_partial(span, ups=ups):
            return mm_cols(b.dpre[0, span, :], ups[0][...]) + mm_cols(b.dpre[1, span, :], ups[1][...])

        scatter(turn, up_partial)
        slots.drop((UP, 0), (UP, 1))
        slots.load((QKVA, 1), r.mats.at[layer, 2])
        slots.load((WATTN, 1), r.foreign_weights.at[layer, 0])
        slots.load(ROWS, r.mats.at[layer, 0])
        slots.load((QKVA, 0), r.mats.at[layer, 1])
        slots.load((WATTN, 0), r.w_attn.at[layer])
        norm_back(turn, layer, 1, normed_copy, inverse_copy, False)
        gather(turn + 1)
        normed_copy = pltpu.make_async_copy(r.norms.at[layer, 0], b.normed, b.misc_sem.at[1])
        normed_copy.start()
        inverse_copy = pltpu.make_async_copy(r.inverses.at[layer, 0], b.inverse, b.misc_sem.at[2])
        inverse_copy.start()
        exchange_wait(turn + 1)
        full = b.full.at[(turn + 1) % 2]
        part_cols = width // 4
        for part in (1, 0):
            wattn, qkva = slots.get((WATTN, part)), slots.get((QKVA, part))
            dqkv = b.dpre.at[part]

            def att_body(i, _, wattn=wattn):
                rows = at(i * 256, 256, 256)
                b.grad_att[rows, :] = mm(full[rows, :], wattn[:, 3 * part_cols :]).astype(BF)
                return 0

            lax.fori_loop(0, length // 256, att_body, 0)
            lse_ref = r.lse.at[layer]
            attend_part_back(
                layer == 0,
                b.grad_att,
                qkva,
                lambda pair, rows, part=part, lse_ref=lse_ref: lse_ref[part, pair, :, rows],
                r.bias,
                dqkv,
                b.dk,
                b.dv,
            )
            summing.advance()
            n_full = slots.get(ROWS)

            def attn_chunk(i, rows, n_full=n_full, dqkv=dqkv, qkva=qkva):
                into_stage(i, mm_rows(n_full[:, rows], dqkv[:, : 3 * part_cols]), slice(0, 3 * part_cols))
                into_stage(i, mm_rows(full[:, rows], qkva[:, 3 * part_cols :]), slice(3 * part_cols, None))

            pending = store_chunks(o.foreign if part == 1 else o.own, base + 2, attn_chunk, pending)
        slots.drop((QKVA, 0), (QKVA, 1), ROWS)
        pending.wait()
        pending = None
        summing.ready = (base + 3) * per_matrix
        summing.feed()
        if layer == 1:
            slots.load((DOWN, 1), r.foreign_weights.at[0, 2])
            slots.load((SLOPE, 1), r.mats.at[0, 7])
            slots.load((ACT, 1), r.mats.at[0, 5])
        summing.advance()
        wattns = [slots.get((WATTN, 0)), slots.get((WATTN, 1))]

        def attn_partial(span, wattns=wattns):
            cols = slice(0, 3 * part_cols)
            return mm_cols(b.dpre[0, span, cols], wattns[0][:, cols]) + mm_cols(
                b.dpre[1, span, cols], wattns[1][:, cols]
            )

        scatter(turn + 1, attn_partial)
        slots.drop((WATTN, 0), (WATTN, 1))
        if layer == 1:
            slots.load(ROWS, r.mats.at[0, 3])
        norm_back(turn + 1, layer, 0, normed_copy, inverse_copy, layer == 0)
        if layer == 1:
            gather(turn + 2)

    other = at((1 - chip) * block, block, block)
    mine = at(chip * block, block, block)
    b.rows_send[...] = b.state[other, :].astype(BF)
    rows_copy = remote(b.rows_send, b.rows_recv, 16, {"tensor": flip(tensor, 2)})
    rows_copy.start()
    small = jnp.zeros(r.sel.shape[:1] + (width,), F32)
    for i in range(8):
        small = small + r.sel[:, i : i + 1] * vec[i : i + 1, :]
    b.small_buf[0, 0] = small

    def small_copy(i):
        return pltpu.make_async_remote_copy(
            src_ref=b.small_buf.at[0, i],
            dst_ref=b.small_buf.at[1, i],
            send_sem=b.small_send.at[i],
            recv_sem=b.small_recv.at[i],
            device_id=partners[i],
            device_id_type=MESH,
        )

    small_copy(0).start()
    for i in range(len(partners)):
        summing.advance()
        small_copy(i).wait()
        total = b.small_buf[0, i] + b.small_buf[1, i]
        if i + 1 < len(partners):
            b.small_buf[0, i + 1] = total
            small_copy(i + 1).start()
        else:
            o.small_out[...] = total
    rows_copy.wait()
    o.frames_grad[chip] = b.state[mine, :]
    o.frames_grad[1 - chip] = b.rows_recv[...].astype(F32)
    summing.drain()


ROWS, DOWN, SLOPE, ACT, UP, QKVA, WATTN = range(7)


class BackIn(NamedTuple):
    grad_in: Any
    mats: Any
    norms: Any
    inverses: Any
    foreign_weights: Any
    w_attn: Any
    w_up: Any
    w_down: Any
    gains: Any
    sel: Any
    bias: Any
    lse: Any


class BackOut(NamedTuple):
    total: Any
    own: Any
    foreign: Any
    landed: Any
    small_out: Any
    frames_grad: Any


class BackScratch(NamedTuple):
    slots: Any
    dpre: Any
    full: Any
    rs_send: Any
    rs_recv: Any
    state: Any
    keep: Any
    normed: Any
    inverse: Any
    stage: Any
    dk: Any
    dv: Any
    grad_att: Any
    vec: Any
    rows_send: Any
    rows_recv: Any
    small_buf: Any
    acc: Any
    seg: Any
    y_view: Any
    own_view: Any
    slot_sem: Any
    misc_sem: Any
    stage_sem: Any
    ex_send: Any
    ex_recv: Any
    small_send: Any
    small_recv: Any
    send_sem: Any
    recv_sem: Any
    copy_sem: Any
    view_sem: Any


def backward(inputs, size):
    half, width = inputs.grad_in.shape
    length = 2 * half
    block = length // 4
    bits = dp_bits(size)
    rows = 256
    matrices = 6
    chunks = matrices * length // rows
    stages = 2 * len(bits) + 1
    ring = min(chunks, 2 * len(bits) + 2)
    steps = halvings(bits, rows, width)
    small_rows = inputs.sel.shape[0]
    exchanges = len(bits) + 2
    whole = jax.ShapeDtypeStruct((chunks, rows, width), BF)
    dma = pltpu.SemaphoreType.DMA
    shapes = BackScratch(
        slots=pltpu.VMEM((5, length, width), BF),
        dpre=pltpu.VMEM((2, length, width), BF),
        full=pltpu.VMEM((2, length, width), BF),
        rs_send=pltpu.VMEM((half, width), BF),
        rs_recv=pltpu.VMEM((2, half, width), BF),
        state=pltpu.VMEM((half, width), F32),
        keep=pltpu.VMEM((half, width), F32),
        normed=pltpu.VMEM((half, width), F32),
        inverse=pltpu.VMEM((half, LANES), F32),
        stage=pltpu.VMEM((length // rows, rows, width), BF),
        dk=pltpu.VMEM((length, LANES), F32),
        dv=pltpu.VMEM((length, LANES), F32),
        grad_att=pltpu.VMEM((length, width // 4), BF),
        vec=pltpu.VMEM((8, width), F32),
        rows_send=pltpu.VMEM((block, width), BF),
        rows_recv=pltpu.VMEM((block, width), BF),
        small_buf=pltpu.VMEM((2, exchanges, small_rows, width), F32),
        acc=pltpu.VMEM((ring, rows, width), BF),
        seg=pltpu.VMEM((chunks,) + steps[-1][:2], BF),
        y_view=pltpu.VMEM((rows, width), BF),
        own_view=pltpu.VMEM((rows, width), BF),
        slot_sem=dma((5,)),
        misc_sem=dma((3,)),
        stage_sem=dma((1,)),
        ex_send=dma((17,)),
        ex_recv=dma((17,)),
        small_send=dma((exchanges,)),
        small_recv=dma((exchanges,)),
        send_sem=dma((stages, chunks)),
        recv_sem=dma((stages, chunks)),
        copy_sem=dma((chunks,)),
        view_sem=dma((2,)),
    )
    scratch = list(shapes)
    scratch += [pltpu.VMEM((ring,) + step[:2], BF) for step in steps]
    any_spec = pl.BlockSpec(memory_space=pl.ANY)
    vmem_spec = pl.BlockSpec(memory_space=pltpu.VMEM)
    outs = pl.pallas_call(
        functools.partial(back_kernel, bits),
        in_specs=[any_spec] * 8 + [vmem_spec] * 4,
        out_specs=[any_spec] * 4 + [vmem_spec] * 2,
        out_shape=[whole] * 4
        + [
            jax.ShapeDtypeStruct((small_rows, width), F32),
            jax.ShapeDtypeStruct((2, block, width), F32),
        ],
        scratch_shapes=scratch,
        compiler_params=pltpu.CompilerParams(
            vmem_limit_bytes=VMEM_BYTES, collective_id=1, has_side_effects=True
        ),
        name="backward",
    )(*inputs)
    total, small, frames_grad = outs[0], outs[4], outs[5]
    return total.reshape(matrices, length, width), small, frames_grad


class Fetching:
    SKEW = 2
    STAGES = 3

    def __init__(self, sources, targets, send_sem, recv_sem):
        self.sources, self.targets = sources, targets
        self.send_sem, self.recv_sem = send_sem, recv_sem
        self.dp = lax.axis_index("dp")
        self.tensor = lax.axis_index("tensor")
        self.half = sources[0].shape[0] // 2
        self.items = 2 * len(sources)
        self.step = 0

    def copies(self, stage, item):
        pieces = []
        for sub in range(2):
            first_bit = 1 + sub
            low = lax.rem(self.dp // first_bit, 2)
            high = lax.rem(self.dp // (3 - first_bit), 2)
            span = self.half // 2
            base = (item % 2) * self.half + sub * span
            quarter = span // 4
            if stage < 2:
                rows = at(base + (2 * high + low) * quarter, quarter, quarter)
            else:
                rows = at(base + high * 2 * quarter, 2 * quarter, 2 * quarter)
            target = self.targets[item // 2].at[rows]
            source = self.sources[item // 2].at[rows] if stage == 0 else target
            if stage == 0:
                device = {"tensor": flip(self.tensor, 2)}
            else:
                device = {"dp": flip(self.dp, first_bit if stage == 1 else 3 - first_bit)}
            pieces.append(
                pltpu.make_async_remote_copy(
                    src_ref=source,
                    dst_ref=target,
                    send_sem=self.send_sem.at[stage, item, sub],
                    recv_sem=self.recv_sem.at[stage, item, sub],
                    device_id=device,
                    device_id_type=MESH,
                )
            )
        return pieces

    def advance(self):
        step = self.step
        for stage in range(self.STAGES, 0, -1):
            item = step - self.SKEW * stage
            if 0 <= item < self.items:
                for copy in self.copies(stage - 1, item):
                    copy.wait_recv()
                if stage < self.STAGES:
                    for copy in self.copies(stage, item):
                        copy.start()
        if step < self.items:
            for copy in self.copies(0, step):
                copy.start()
        self.step += 1

    def need(self, matrix):
        while self.step <= 2 * matrix + 1 + self.SKEW * self.STAGES:
            self.advance()

    def drain(self):
        self.need(len(self.sources) - 1)
        for item in range(self.items):
            for stage in range(self.STAGES):
                for copy in self.copies(stage, item):
                    copy.wait_send()


def forward_kernel(bits, *refs):
    r, refs = ForwardIn(*refs[: len(ForwardIn._fields)]), refs[len(ForwardIn._fields) :]
    o, refs = ForwardOut(*refs[: len(ForwardOut._fields)]), refs[len(ForwardOut._fields) :]
    b = ForwardScratch(*refs)
    dp = lax.axis_index("dp")
    tensor = lax.axis_index("tensor")
    chip = tensor // 2
    core = lax.rem(tensor, 2)
    half, width = b.state.shape
    length = 2 * half
    block = length // 4
    part_cols = width // 4
    core_partner = {"tensor": flip(tensor, 1)}
    chip_partner = {"tensor": flip(tensor, 2)}
    partners = [core_partner, chip_partner] + [{"dp": flip(dp, bit)} for bit in bits[:2]]

    barrier = pltpu.get_barrier_semaphore()
    for partner in partners:
        pl.semaphore_signal(barrier, inc=1, device_id=partner, device_id_type=MESH)
    pl.semaphore_wait(barrier, len(partners))

    def remote(source, target, sem, device):
        return pltpu.make_async_remote_copy(
            src_ref=source,
            dst_ref=target,
            send_sem=b.ex_send.at[sem],
            recv_sem=b.ex_recv.at[sem],
            device_id=device,
            device_id_type=MESH,
        )

    def local(source, target, sem):
        return pltpu.make_async_copy(source, target, b.local_sem.at[sem])

    frames_copy = remote(r.frames.at[1 - chip], b.frames_got, 16, chip_partner)
    frames_copy.start()
    own_copy = local(r.frames.at[chip], b.frames_own, 0)
    own_copy.start()
    slots = Slots(b.slots, b.slot_sem)
    slots.load((WATTN, 0), r.w_attn.at[0])
    sources, targets = [], []
    for layer in range(2):
        sources += [r.w_attn.at[layer], r.w_up.at[layer], r.w_down.at[layer]]
        targets += [o.foreign_weights.at[layer, i] for i in range(3)]
    fetching = Fetching(sources, targets, b.send_sem, b.recv_sem)
    fetching.advance()
    fetching.advance()
    own_copy.wait()
    frames_copy.wait()
    b.state[at(chip * block, block, block), :] = b.frames_own[...].astype(F32)
    b.state[at((1 - chip) * block, block, block), :] = b.frames_got[...].astype(F32)
    grad_copy = remote(r.out_grad.at[1 - chip], b.grad_got, 17, chip_partner)
    grad_copy.start()
    grad_own_copy = local(r.out_grad.at[chip], b.grad_own, 0)
    grad_own_copy.start()

    def exchange_copies(turn):
        full = b.full.at[turn % 2]
        spans = [at((2 * j + core) * block, block, block) for j in range(2)]
        return [remote(full.at[s], full.at[s], 4 * turn + j, core_partner) for j, s in enumerate(spans)]

    def scatter(turn, partial):
        copies = [
            remote(
                b.rs_send.at[pl.ds(j * block, block)],
                b.rs_recv.at[turn % 2, pl.ds(j * block, block)],
                4 * turn + 2 + j,
                core_partner,
            )
            for j in range(2)
        ]
        for j in range(2):
            span = at((2 * j + 1 - core) * block, block, block)
            b.rs_send[pl.ds(j * block, block), :] = partial(span).astype(BF)
            copies[j].start()
        for j in range(2):
            span = at((2 * j + core) * block, block, block)
            b.keep[pl.ds(j * block, block), :] = partial(span)
        for copy in copies:
            copy.wait()

    norm_copies = []

    def norm(turn, layer, which, add):
        for copy in norm_copies:
            copy.wait()
        norm_copies.clear()
        gain = r.gains[2 * layer + which : 2 * layer + which + 1, :]
        shift = r.shifts[2 * layer + which : 2 * layer + which + 1, :]
        step = 128
        copies = exchange_copies(turn)
        for j in range(2):

            def rows_body(i, _, j=j):
                span = at(j * block + i * step, step, step)
                state = b.state[span, :]
                if add:
                    state = state + (b.keep[span, :] + b.rs_recv[(turn - 1) % 2, span, :].astype(F32))
                    b.state[span, :] = state
                centred = state - jnp.mean(state, axis=-1, keepdims=True)
                variance = jnp.mean(centred * centred, axis=-1, keepdims=True)
                inverse = lax.rsqrt(variance + 1e-05)
                normed = centred * inverse
                b.normed[span, :] = normed
                b.inverse[span, :] = jnp.broadcast_to(inverse, (step, LANES))
                b.full[turn % 2, at((2 * j + core) * block + i * step, step, step), :] = (
                    normed * gain + shift
                ).astype(BF)
                return 0

            lax.fori_loop(0, block // step, rows_body, 0)
            copies[j].start()
        norm_copies.append(local(b.normed, o.norms.at[layer, which], 1))
        norm_copies.append(local(b.inverse, o.inverses.at[layer, which], 2))
        for copy in norm_copies:
            copy.start()
        for copy in copies:
            copy.wait()

    saves = []

    def save(source, target, sem):
        copy = local(source, target, sem)
        copy.start()
        saves.append(copy)

    def settle():
        for copy in saves:
            copy.wait()
        saves.clear()

    for layer in range(2):
        turn = 2 * layer
        norm(turn, layer, 0, layer == 1)
        full = b.full.at[turn % 2]
        settle()
        save(full, o.mats.at[layer, 0], 3)
        fetching.advance()
        for part in range(2):
            if part == 1:
                fetching.need(3 * layer)
                slots.load((WATTN, 1), o.foreign_weights.at[layer, 0])
            attend_part(
                layer == 0, full, slots.get((WATTN, part)), r.bias, b.acts.at[part], o.lse.at[layer, part]
            )
            save(b.acts.at[part], o.mats.at[layer, 1 + part], 4 + part)
            if part == 0:
                slots.load((UP, 0), r.w_up.at[layer])
                slots.load((DOWN, 0), r.w_down.at[layer])
            fetching.advance()
        weights = [slots.get((WATTN, part)) for part in range(2)]

        def out_partial(span, weights=weights):
            cols = slice(3 * part_cols, None)
            return mm_cols(b.acts[0, span, cols], weights[0][:, cols]) + mm_cols(
                b.acts[1, span, cols], weights[1][:, cols]
            )

        scatter(turn, out_partial)
        slots.drop((WATTN, 0), (WATTN, 1))
        fetching.advance()
        turn += 1
        norm(turn, layer, 1, True)
        full = b.full.at[turn % 2]
        settle()
        save(full, o.mats.at[layer, 3], 3)
        fetching.advance()
        for part in range(2):
            if part == 1:
                fetching.need(3 * layer + 1)
                slots.load((UP, 1), o.foreign_weights.at[layer, 1])
            up = slots.get((UP, part))

            def up_body(i, _, part=part, up=up, full=full):
                rows = at(i * 256, 256, 256)
                for first in range(0, width, 256):
                    cols = pl.ds(first, 256)
                    active, slope = gelu_parts(mm(full[rows, :], up[:, cols]))
                    b.acts[part, rows, cols] = active.astype(BF)
                    b.slope[part, rows, cols] = slope.astype(BF)
                return 0

            lax.fori_loop(0, length // 256, up_body, 0)
            save(b.acts.at[part], o.mats.at[layer, 4 + part], 4 + part)
            save(b.slope.at[part], o.mats.at[layer, 6 + part], 6 + part)
            slots.drop((UP, part))
            if part == 0 and layer == 0:
                slots.load((WATTN, 0), r.w_attn.at[1])
            fetching.advance()
        fetching.need(3 * layer + 2)
        slots.load((DOWN, 1), o.foreign_weights.at[layer, 2])
        downs = [slots.get((DOWN, part)) for part in range(2)]

        def down_partial(span, downs=downs):
            return mm(b.acts[0, span, :], downs[0][...]) + mm(b.acts[1, span, :], downs[1][...])

        scatter(turn, down_partial)
        slots.drop((DOWN, 0), (DOWN, 1))
        if layer == 0:
            fetching.advance()

    for j in range(2):
        span = pl.ds(j * block, block)
        total = b.state[span, :] + (b.keep[span, :] + b.rs_recv[1, span, :].astype(F32))
        b.hidden[j] = total.astype(BF)
    hidden_copy = remote(b.hidden.at[1 - chip], b.hidden_got, 18, chip_partner)
    hidden_copy.start()
    grad_own_copy.wait()
    grad_copy.wait()
    o.grad_in[at(chip * block, block, block), :] = b.grad_own[...].astype(F32)
    o.grad_in[at((1 - chip) * block, block, block), :] = b.grad_got[...].astype(F32)
    fetching.drain()
    settle()
    for copy in norm_copies:
        copy.wait()
    hidden_copy.wait()
    o.hidden_out[chip] = b.hidden[chip]
    o.hidden_out[1 - chip] = b.hidden_got[...]


class ForwardIn(NamedTuple):
    frames: Any
    out_grad: Any
    w_attn: Any
    w_up: Any
    w_down: Any
    gains: Any
    shifts: Any
    bias: Any


class ForwardOut(NamedTuple):
    mats: Any
    norms: Any
    inverses: Any
    foreign_weights: Any
    lse: Any
    grad_in: Any
    hidden_out: Any


class ForwardScratch(NamedTuple):
    slots: Any
    acts: Any
    slope: Any
    full: Any
    rs_send: Any
    rs_recv: Any
    state: Any
    keep: Any
    normed: Any
    inverse: Any
    frames_own: Any
    frames_got: Any
    grad_own: Any
    grad_got: Any
    hidden: Any
    hidden_got: Any
    slot_sem: Any
    local_sem: Any
    ex_send: Any
    ex_recv: Any
    send_sem: Any
    recv_sem: Any


def forward(inputs, size):
    block, width = inputs.frames.shape[1:]
    half, length = 2 * block, 4 * block
    bits = dp_bits(size)
    dma = pltpu.SemaphoreType.DMA
    rows = pltpu.VMEM((block, width), BF)
    scratch = ForwardScratch(
        slots=pltpu.VMEM((5, length, width), BF),
        acts=pltpu.VMEM((2, length, width), BF),
        slope=pltpu.VMEM((2, length, width), BF),
        full=pltpu.VMEM((2, length, width), BF),
        rs_send=pltpu.VMEM((half, width), BF),
        rs_recv=pltpu.VMEM((2, half, width), BF),
        state=pltpu.VMEM((half, width), F32),
        keep=pltpu.VMEM((half, width), F32),
        normed=pltpu.VMEM((half, width), F32),
        inverse=pltpu.VMEM((half, LANES), F32),
        frames_own=rows,
        frames_got=rows,
        grad_own=rows,
        grad_got=rows,
        hidden=pltpu.VMEM((2, block, width), BF),
        hidden_got=rows,
        slot_sem=dma((5,)),
        local_sem=dma((8,)),
        ex_send=dma((19,)),
        ex_recv=dma((19,)),
        send_sem=dma((3, 12, 2)),
        recv_sem=dma((3, 12, 2)),
    )
    out_shape = ForwardOut(
        mats=jax.ShapeDtypeStruct((2, 8, length, width), BF),
        norms=jax.ShapeDtypeStruct((2, 2, half, width), F32),
        inverses=jax.ShapeDtypeStruct((2, 2, half, LANES), F32),
        foreign_weights=jax.ShapeDtypeStruct((2, 3, length, width), BF),
        lse=jax.ShapeDtypeStruct((2, 2, width // (4 * LANES), 8, length), F32),
        grad_in=jax.ShapeDtypeStruct((half, width), F32),
        hidden_out=jax.ShapeDtypeStruct((2, block, width), BF),
    )
    any_spec = pl.BlockSpec(memory_space=pl.ANY)
    vmem_spec = pl.BlockSpec(memory_space=pltpu.VMEM)
    outs = pl.pallas_call(
        functools.partial(forward_kernel, bits),
        in_specs=[any_spec] * 5 + [vmem_spec] * 3,
        out_specs=[any_spec] * 4 + [vmem_spec] * 3,
        out_shape=list(out_shape),
        scratch_shapes=list(scratch),
        compiler_params=pltpu.CompilerParams(
            vmem_limit_bytes=VMEM_BYTES, collective_id=2, has_side_effects=True
        ),
        name="forward",
    )(*inputs)
    return ForwardOut(*outs)


def per_device(
    frames, lengths, codebook, ln_gain, ln_bias, ada_scale, ada_shift, w_qkv, w_out, w_up, w_down, out_grad
):
    chip = lax.axis_index("tensor") // 2
    length = frames.shape[1] * lax.axis_size("tensor")
    size = lax.axis_size("dp")

    def pick(pair):
        return jnp.where(chip == 0, pair[0], pair[1])

    bias = jnp.where(jnp.arange(length) < pick(lengths), 0.0, -1e30).astype(F32)
    sections = ada_scale.shape[0]
    chosen = (jnp.arange(sections) == pick(codebook))[:, None, None]
    gains = jnp.concatenate([ln_gain, jnp.sum(jnp.where(chosen, ada_scale, 0.0), axis=0)])
    shifts = jnp.concatenate([ln_bias, jnp.sum(jnp.where(chosen, ada_shift, 0.0), axis=0)])
    w_attn = jnp.concatenate(
        [w_qkv.reshape(w_qkv.shape[0], w_qkv.shape[1], -1), w_out.transpose(0, 2, 1)], axis=2
    )
    ahead = forward(
        ForwardIn(frames, out_grad, w_attn, w_up, w_down, gains, shifts, bias[None, :]), size
    )
    unit = jnp.eye(8, dtype=F32)
    sel = jnp.concatenate(
        [unit[0:3:2], unit[1:4:2]]
        + [jnp.where(chosen, rows[None], 0.0).reshape(2 * sections, 8) for rows in (unit[4:7:2], unit[5:8:2])]
    )
    total, small, frames_grad = backward(
        BackIn(
            ahead.grad_in,
            ahead.mats,
            ahead.norms,
            ahead.inverses,
            ahead.foreign_weights,
            w_attn,
            w_up,
            w_down,
            gains,
            sel,
            bias[:, None],
            ahead.lse,
        ),
        size,
    )
    total = total.reshape((2, 3) + total.shape[1:])
    wide = w_qkv.shape[2] * w_qkv.shape[3]
    return (
        ahead.hidden_out,
        frames_grad,
        small[0:2],
        small[2:4],
        small[4 : 4 + 2 * sections].reshape(ada_scale.shape),
        small[4 + 2 * sections :].reshape(ada_scale.shape),
        total[::-1, 2, :, :wide].reshape(w_qkv.shape).astype(F32),
        total[::-1, 2, :, wide:].transpose(0, 2, 1).astype(F32),
        total[::-1, 1].astype(F32),
        total[::-1, 0].astype(F32),
    )


def solution(mesh):
    placed = (
        P("dp", "tensor", None),
        P("dp"),
        P("dp"),
        P(),
        P(),
        P(),
        P(),
        P(None, None, None, "tensor"),
        P(None, "tensor", None),
        P(None, None, "tensor"),
        P(None, "tensor", None),
        P("dp", "tensor", None),
    )
    return jax.shard_map(
        per_device,
        mesh=mesh,
        in_specs=placed,
        out_specs=(
            P("dp", "tensor", None),
            P("dp", "tensor", None),
            P(),
            P(),
            P(),
            P(),
            P(None, None, None, "tensor"),
            P(None, "tensor", None),
            P(None, None, "tensor"),
            P(None, "tensor", None),
        ),
        check_vma=False,
    )
```

```python
import functools
from typing import Any, NamedTuple

import jax
import jax.numpy as jnp
from jax import lax
from jax.experimental import pallas as pl
from jax.experimental.pallas import tpu as pltpu
from jax.sharding import PartitionSpec as P

HEAD_DIM = 64
BF = jnp.bfloat16
F32 = jnp.float32
HIGH = lax.Precision.HIGHEST
MESH = pl.DeviceIdType.MESH
VMEM_BYTES = 60 << 20
LANES = 128


def mm(left, right):
    return jnp.dot(left, right, preferred_element_type=F32)


def mm_rows(left, right):
    return lax.dot_general(left, right, (((0,), (0,)), ((), ())), preferred_element_type=F32)


def mm_cols(left, right, precision=None):
    return lax.dot_general(
        left, right, (((1,), (1,)), ((), ())), precision=precision, preferred_element_type=F32
    )


def head_of_lane(shape):
    return lax.broadcasted_iota(jnp.int32, shape, len(shape) - 1) // HEAD_DIM


def at(start, size, unit):
    return pl.ds(pl.multiple_of(start, unit), size)


def flip(index, bit):
    return index + bit - 2 * bit * lax.rem(index // bit, 2)


def dp_bits(size):
    bits = []
    while 2 ** len(bits) < size:
        bits.append(2 ** len(bits))
    return bits


def attend_part(causal, n_ref, w_ref, bias_ref, qkva_ref, lse_ref, between):
    length = n_ref.shape[0]
    part = qkva_ref.shape[1] // 4
    block = length // 4
    scaling = HEAD_DIM ** (-0.5)

    def project(index, _):
        rows = at(index * block, block, block)
        qkva_ref[rows, : 3 * part] = mm(n_ref[rows, :], w_ref[:, : 3 * part]).astype(BF)
        return 0

    lax.fori_loop(0, 4, project, 0)

    for pair in range(part // LANES):
        q_cols, k_cols, v_cols, a_cols = [pl.ds(i * part + pair * LANES, LANES) for i in range(4)]
        for first in range(0, length, block):
            rows = pl.ds(first, block)
            reach = first + block if causal else length
            queries = qkva_ref[rows, q_cols] * jnp.asarray(scaling, BF)
            keys = qkva_ref[pl.ds(0, reach), k_cols]
            values = qkva_ref[pl.ds(0, reach), v_cols]
            bias = bias_ref[:, pl.ds(0, reach)]
            head = head_of_lane(queries.shape)
            lanes = lax.broadcasted_iota(jnp.int32, (block, LANES), 1)
            mixed = None
            stats = jnp.zeros((block, LANES), F32)
            for which in range(2):
                scores = mm_cols(jnp.where(head == which, queries, jnp.zeros_like(queries)), keys) + bias
                if causal:
                    query_at = lax.broadcasted_iota(jnp.int32, (block, block), 0)
                    key_at = lax.broadcasted_iota(jnp.int32, (block, block), 1)
                    last = jnp.where(key_at <= query_at, scores[:, first:], -1e30)
                    scores = jnp.concatenate([scores[:, :first], last], axis=1) if first else last
                row_max = jnp.max(scores, axis=-1, keepdims=True)
                raised = jnp.exp(scores - row_max)
                total = jnp.sum(raised, axis=-1, keepdims=True)
                one = mm(raised.astype(BF), values) * (1.0 / total)
                mixed = one if mixed is None else jnp.where(head == 0, mixed, one)
                stats = jnp.where(lanes == which, row_max + jnp.log(total), stats)
            qkva_ref[rows, a_cols] = mixed.astype(BF)
            square = lax.broadcasted_iota(jnp.int32, (8, LANES), 1)
            pick = (square == lax.broadcasted_iota(jnp.int32, (8, LANES), 0)).astype(F32)
            lse_ref[pair, :, rows] = mm_cols(pick, stats, HIGH)
        between()


def attend_part_back(causal, grad_att_ref, qkva_ref, lse_of, bias_ref, dqkv_ref, dk_ref, dv_ref, between):
    length = qkva_ref.shape[0]
    part = qkva_ref.shape[1] // 4
    block = length // 4
    scaling = HEAD_DIM ** (-0.5)

    for pair in range(part // LANES):
        q_cols, k_cols, v_cols, a_cols = [pl.ds(i * part + pair * LANES, LANES) for i in range(4)]
        g_cols = pl.ds(pair * LANES, LANES)
        dk_ref[...] = jnp.zeros_like(dk_ref)
        dv_ref[...] = jnp.zeros_like(dv_ref)
        keys_turned = qkva_ref[:, k_cols].astype(F32).T.astype(BF)
        feature = lax.broadcasted_iota(jnp.int32, keys_turned.shape, 0) // HEAD_DIM
        turned = [
            jnp.where(feature == which, keys_turned, jnp.zeros_like(keys_turned)) for which in range(2)
        ]
        for first in range(0, length, block):
            rows = pl.ds(first, block)
            reach = first + block if causal else length
            queries = qkva_ref[rows, q_cols] * jnp.asarray(scaling, BF)
            grads = grad_att_ref[rows, g_cols]
            head = head_of_lane(queries.shape)
            pick = (head_of_lane((8, LANES)) == lax.broadcasted_iota(jnp.int32, (8, LANES), 0)).astype(F32)
            product = grads.astype(F32) * qkva_ref[rows, a_cols].astype(F32)
            delta = mm_cols(pick, product, HIGH)
            lse = lse_of(pair, rows)
            keys = qkva_ref[pl.ds(0, reach), k_cols]
            values = qkva_ref[pl.ds(0, reach), v_cols]
            bias = bias_ref[pl.ds(0, reach), :]
            dq_turned = None
            for which in range(2):
                queries_one = jnp.where(head == which, queries, jnp.zeros_like(queries))
                grads_one = jnp.where(head == which, grads, jnp.zeros_like(grads))
                scores = mm_cols(keys, queries_one) + bias
                if causal:
                    key_at = lax.broadcasted_iota(jnp.int32, (block, block), 0)
                    query_at = lax.broadcasted_iota(jnp.int32, (block, block), 1)
                    last = jnp.where(key_at <= query_at, scores[first:], -1e30)
                    scores = jnp.concatenate([scores[:first], last], axis=0) if first else last
                probs = jnp.exp(scores - lse[which : which + 1])
                grad_probs = mm_cols(values, grads_one)
                grad_scores = (probs * (grad_probs - delta[which : which + 1])).astype(BF)
                dv_ref[pl.ds(0, reach), :] += mm(probs.astype(BF), grads_one)
                dk_ref[pl.ds(0, reach), :] += mm(grad_scores, queries_one)
                one = mm(turned[which][:, :reach], grad_scores)
                dq_turned = one if dq_turned is None else dq_turned + one
            dqkv_ref[rows, q_cols] = (dq_turned.T * scaling).astype(BF)
        dqkv_ref[:, k_cols] = dk_ref[...].astype(BF)
        dqkv_ref[:, v_cols] = dv_ref[...].astype(BF)
        between()


def gelu_parts(hidden):
    bell = jnp.exp(-0.5 * hidden * hidden)
    base = 1.0 + 0.23164189 * jnp.abs(hidden)
    t = pl.reciprocal(base, approx=True)
    t = t * (2.0 - base * t)
    poly = 0.5307027145
    poly = poly * t - 0.7265760135
    poly = poly * t + 0.7107068705
    poly = poly * t - 0.142248368
    poly = poly * t + 0.127414796
    tail = poly * t * bell
    cdf = jnp.where(hidden >= 0, 1.0 - tail, tail)
    return hidden * cdf, cdf + hidden * bell * 0.3989422804014327


class Slots:
    def __init__(self, buffers, sems):
        self.buffers = buffers
        self.sems = sems
        self.free = list(range(buffers.shape[0]))
        self.held = {}

    def load(self, name, source):
        slot = self.free.pop(0)
        copy = pltpu.make_async_copy(source, self.buffers.at[slot], self.sems.at[slot])
        copy.start()
        self.held[name] = [slot, copy]

    def get(self, name):
        slot, copy = self.held[name]
        if copy is not None:
            copy.wait()
            self.held[name][1] = None
        return self.buffers.at[slot]

    def reserve(self, name):
        slot = self.free.pop(0)
        self.held[name] = [slot, None]
        return self.buffers.at[slot]

    def rename(self, old, new):
        self.held[new] = self.held.pop(old)

    def drop(self, *names):
        for name in names:
            self.free.append(self.held.pop(name)[0])


class Summing:
    AHEAD = 4

    def __init__(self, bits, own, foreign, outs, acc, seg, own_view, rbufs, send_sem, recv_sem, copy_sem, view_sem):
        self.bits, self.own, self.foreign, self.outs = bits, own, foreign, outs
        self.acc, self.seg, self.own_view, self.rbufs = acc, seg, own_view, rbufs
        self.send_sem, self.recv_sem, self.copy_sem, self.view_sem = send_sem, recv_sem, copy_sem, view_sem
        self.chunks, self.rows, self.columns = own.shape
        self.ring = acc.shape[0]
        self.stages = 2 * len(bits) + 1
        self.dp = lax.axis_index("dp")
        self.tensor = lax.axis_index("tensor")
        self.step = 0
        self.started = 0
        self.ready = 0
        self.sizes = [step[:2] for step in halvings(bits, self.rows, self.columns)]
        row, column = 0, 0
        self.plan = []
        for half_rows, half_columns, bit, by_rows in halvings(bits, self.rows, self.columns):
            flag = lax.rem(self.dp // bit, 2)
            if by_rows:
                keep = (row + flag * half_rows, column)
                send = (row + (1 - flag) * half_rows, column)
            else:
                keep = (row, column + flag * half_columns)
                send = (row, column + (1 - flag) * half_columns)
            row, column = keep
            self.plan.append((keep, send, bit))

    def region(self, where, size):
        return at(where[0], size[0], 16), at(where[1], size[1], LANES)

    def place(self, c):
        per_matrix = self.outs[0].shape[1]
        matrix = c // per_matrix
        return self.outs[matrix % 3].at[1 - matrix // 3, c % per_matrix]

    def copy(self, s, c):
        count = len(self.bits)
        slot = c % self.ring
        if s == 0:
            source, target = self.foreign.at[c], self.acc.at[slot]
            device = {"tensor": flip(self.tensor, 2)}
        elif s <= count:
            i = s - 1
            _, send, bit = self.plan[i]
            rows, columns = self.region(send, self.sizes[i])
            source = self.acc.at[slot, rows, columns]
            target, device = self.rbufs[i].at[slot], {"dp": flip(self.dp, bit)}
        else:
            i = 2 * count - s
            keep, _, bit = self.plan[i]
            rows, columns = self.region(keep, self.sizes[i])
            target = self.place(c).at[rows, columns]
            source = self.seg.at[c] if i == count - 1 else target
            device = {"dp": flip(self.dp, bit)}
        return pltpu.make_async_remote_copy(
            src_ref=source,
            dst_ref=target,
            send_sem=self.send_sem.at[s, c],
            recv_sem=self.recv_sem.at[s, c],
            device_id=device,
            device_id_type=MESH,
        )

    def seg_copy(self, c):
        rows, columns = self.region(self.plan[-1][0], self.sizes[-1])
        return pltpu.make_async_copy(self.seg.at[c], self.place(c).at[rows, columns], self.copy_sem.at[c])

    def view(self, c):
        return pltpu.make_async_copy(self.own.at[c], self.own_view.at[c % 2], self.view_sem.at[c % 2])

    def finish(self, s, c):
        count = len(self.bits)
        slot = c % self.ring
        self.copy(s, c).wait_recv()
        if s == 0:
            self.view(c).wait()
            self.acc[slot] = (self.own_view[c % 2].astype(F32) + self.acc[slot].astype(F32)).astype(BF)
        elif s <= count:
            i = s - 1
            rows, columns = self.region(self.plan[i][0], self.sizes[i])
            total = self.acc[slot, rows, columns].astype(F32) + self.rbufs[i][slot].astype(F32)
            if s == count:
                self.seg[c] = total.astype(BF)
                self.seg_copy(c).start()
                for stage in range(1, count + 1):
                    self.copy(stage, c).wait_send()
            else:
                self.acc[slot, rows, columns] = total.astype(BF)
        elif s == count + 1:
            self.seg_copy(c).wait()

    def advance(self):
        step = self.step
        if step < self.chunks:
            self.view(step).start()
        for s in range(self.stages - 1, -1, -1):
            c = step - s
            if 0 <= c < self.chunks:
                self.finish(s, c)
                if s + 1 < self.stages:
                    self.copy(s + 1, c).start()
        self.step += 1
        self.feed()

    def feed(self):
        ahead = self.AHEAD if self.step < self.chunks // 2 else 2
        while self.started < min(self.ready, self.step + ahead):
            self.copy(0, self.started).start()
            self.started += 1

    def drain(self):
        while self.step < self.chunks + self.stages - 1:
            self.advance()
        count = len(self.bits)
        for c in range(self.chunks):
            for s in range(self.stages):
                if not 1 <= s <= count:
                    self.copy(s, c).wait_send()


def halvings(bits, rows, columns):
    steps = []
    for bit in bits:
        by_rows = rows >= 32
        rows, columns = (rows // 2, columns) if by_rows else (rows, columns // 2)
        steps.append((rows, columns, bit, by_rows))
    return steps


def back_kernel(bits, *refs):
    r, refs = BackIn(*refs[: len(BackIn._fields)]), refs[len(BackIn._fields) :]
    o, refs = BackOut(*refs[: len(BackOut._fields)]), refs[len(BackOut._fields) :]
    b, rbufs = BackScratch(*refs[: len(BackScratch._fields)]), refs[len(BackScratch._fields) :]
    dp = lax.axis_index("dp")
    tensor = lax.axis_index("tensor")
    chip = tensor // 2
    core = lax.rem(tensor, 2)
    half, width = b.state.shape
    length = 2 * half
    block = length // 4
    core_partner = {"tensor": flip(tensor, 1)}
    partners = [core_partner, {"tensor": flip(tensor, 2)}] + [{"dp": flip(dp, bit)} for bit in bits]

    barrier = pltpu.get_barrier_semaphore()
    for partner in partners:
        pl.semaphore_signal(barrier, inc=1, device_id=partner, device_id_type=MESH)
    pl.semaphore_wait(barrier, len(partners))

    slots = Slots(b.slots, b.slot_sem)
    summing = Summing(
        bits, o.own, o.foreign, (o.down, o.up, o.attn), b.acc, b.seg, b.own_view,
        rbufs, b.send_sem, b.recv_sem, b.copy_sem, b.view_sem,
    )
    per_matrix = length // summing.rows
    vec = b.vec
    vec[...] = jnp.zeros_like(vec)

    def remote(source, target, sem, device):
        return pltpu.make_async_remote_copy(
            src_ref=source,
            dst_ref=target,
            send_sem=b.ex_send.at[sem],
            recv_sem=b.ex_recv.at[sem],
            device_id=device,
            device_id_type=MESH,
        )

    def exchange_copies(turn):
        full = b.full.at[turn % 2]
        spans = [at((2 * j + core) * block, block, block) for j in range(2)]
        return [remote(full.at[s], full.at[s], 4 * turn + j, core_partner) for j, s in enumerate(spans)]

    def exchange_start(turn, j):
        exchange_copies(turn)[j].start()

    def exchange_wait(turn):
        for copy in exchange_copies(turn):
            copy.wait()

    def scatter_copies(turn):
        return [
            remote(
                b.rs_send.at[pl.ds(j * block, block)],
                b.rs_recv.at[turn % 2, pl.ds(j * block, block)],
                4 * turn + 2 + j,
                core_partner,
            )
            for j in range(2)
        ]

    def scatter(turn, partial):
        copies = scatter_copies(turn)
        for j in range(2):
            span = at((2 * j + 1 - core) * block, block, block)
            b.rs_send[pl.ds(j * block, block), :] = partial(span).astype(BF)
            copies[j].start()
        for j in range(2):
            span = at((2 * j + core) * block, block, block)
            b.keep[pl.ds(j * block, block), :] = partial(span)
        for copy in copies:
            copy.wait()

    def norm_back(turn, layer, which, normed_copy, inverse_copy, last):
        normed_copy.wait()
        inverse_copy.wait()
        index = 4 * layer + 2 * which
        gain = r.gains[2 * layer + which : 2 * layer + which + 1, :]
        step = 128

        def rows_body(i, _):
            span = at(i * step, step, step)
            grad = b.keep[span, :] + b.rs_recv[turn % 2, span, :].astype(F32)
            normed = b.normed[span, :]
            moved = grad * gain
            mean_grad = jnp.mean(moved, axis=-1, keepdims=True)
            mean_proj = jnp.mean(moved * normed, axis=-1, keepdims=True)
            state = b.state[span, :] + b.inverse[span, :1] * (moved - mean_grad - normed * mean_proj)
            b.state[span, :] = state
            vec[index : index + 1, :] += jnp.sum(grad * normed, axis=0, keepdims=True)
            vec[index + 1 : index + 2, :] += jnp.sum(grad, axis=0, keepdims=True)
            return 0

        lax.fori_loop(0, half // step, rows_body, 0)

    def gather(turn):
        for j in range(2):
            span = at((2 * j + core) * block, block, block)
            b.full[turn % 2, span, :] = b.state[pl.ds(j * block, block), :].astype(BF)
            exchange_start(turn, j)

    def store_chunks(where, matrix, chunk_of, previous):
        if previous is not None:
            previous.wait()
        stage = b.stage

        def body(i, _):
            chunk_of(i, at(i * summing.rows, summing.rows, summing.rows))
            return 0

        lax.fori_loop(0, per_matrix, body, 0)
        copy = pltpu.make_async_copy(
            stage, where.at[pl.ds(matrix * per_matrix, per_matrix)], b.stage_sem.at[0]
        )
        copy.start()
        return copy

    def into_stage(i, value, columns=slice(None)):
        b.stage[i, :, columns] = value.astype(BF)

    hidden_copy = remote(r.hidden.at[1 - chip], o.hidden_out.at[chip], 17, {"tensor": flip(tensor, 2)})
    hidden_copy.start()
    hidden_own_copy = pltpu.make_async_copy(r.hidden.at[chip], o.hidden_out.at[chip], b.misc_sem.at[3])
    hidden_own_copy.start()
    state_copy = pltpu.make_async_copy(r.grad_in, b.state, b.misc_sem.at[0])
    state_copy.start()
    slots.load((DOWN, 1), r.foreign_weights.at[1, 2])
    slots.load((SLOPE, 1), r.mats.at[1, 7])
    slots.load((ACT, 1), r.mats.at[1, 5])
    slots.load(ROWS, r.mats.at[1, 3])
    state_copy.wait()
    gather(0)
    pending = None

    for layer in (1, 0):
        base = 0 if layer == 1 else 3
        turn = 0 if layer == 1 else 2
        exchange_wait(turn)
        full = b.full.at[turn % 2]
        normed_copy = pltpu.make_async_copy(r.norms.at[layer, 1], b.normed, b.misc_sem.at[1])
        normed_copy.start()
        inverse_copy = pltpu.make_async_copy(r.inverses.at[layer, 1], b.inverse, b.misc_sem.at[2])
        inverse_copy.start()
        for part in (1, 0):
            where = o.foreign if part == 1 else o.own
            act, n_full = slots.get((ACT, part)), slots.get(ROWS)
            dpre = b.dpre.at[part]

            def down_chunk(i, rows, act=act):
                into_stage(i, mm_rows(act[:, rows], full[...]))

            def up_chunk(i, rows, n_full=n_full, dpre=dpre):
                into_stage(i, mm_rows(n_full[:, rows], dpre[...]))

            pending = store_chunks(where, base, down_chunk, pending)
            slots.drop((ACT, part))
            if part == 1:
                slots.load((ACT, 0), r.mats.at[layer, 4])
            else:
                slots.load((UP, 1), r.foreign_weights.at[layer, 1])
            down, slope = slots.get((DOWN, part)), slots.get((SLOPE, part))

            def slope_body(i, _, down=down, slope=slope, dpre=dpre):
                rows = at(i * 256, 256, 256)
                dpre[rows, :] = (mm_cols(full[rows, :], down[...]) * slope[rows, :].astype(F32)).astype(BF)
                return 0

            if part == 1:
                pending.wait()
                pending = None
                summing.ready = (base + 1) * per_matrix
                summing.feed()
            lax.fori_loop(0, length // 256, slope_body, 0)
            slots.drop((DOWN, part), (SLOPE, part))
            if part == 1:
                slots.load((DOWN, 0), r.w_down.at[layer])
                slots.load((SLOPE, 0), r.mats.at[layer, 6])
            else:
                slots.load((UP, 0), r.w_up.at[layer])
            pending = store_chunks(where, base + 1, up_chunk, pending)
            if part == 1:
                pending.wait()
                pending = None
                summing.ready = (base + 2) * per_matrix
                summing.feed()
            if layer == 0:
                summing.advance()
        slots.drop(ROWS)
        pending.wait()
        pending = None
        summing.advance()
        ups = [slots.get((UP, 0)), slots.get((UP, 1))]

        def up_partial(span, ups=ups):
            return mm_cols(b.dpre[0, span, :], ups[0][...]) + mm_cols(b.dpre[1, span, :], ups[1][...])

        scatter(turn, up_partial)
        slots.drop((UP, 0), (UP, 1))
        slots.load((QKVA, 1), r.mats.at[layer, 2])
        slots.load((WATTN, 1), r.foreign_weights.at[layer, 0])
        slots.load(ROWS, r.mats.at[layer, 0])
        slots.load((QKVA, 0), r.mats.at[layer, 1])
        slots.load((WATTN, 0), r.w_attn.at[layer])
        norm_back(turn, layer, 1, normed_copy, inverse_copy, False)
        gather(turn + 1)
        summing.advance()
        normed_copy = pltpu.make_async_copy(r.norms.at[layer, 0], b.normed, b.misc_sem.at[1])
        normed_copy.start()
        inverse_copy = pltpu.make_async_copy(r.inverses.at[layer, 0], b.inverse, b.misc_sem.at[2])
        inverse_copy.start()
        exchange_wait(turn + 1)
        full = b.full.at[(turn + 1) % 2]
        part_cols = width // 4
        for part in (1, 0):
            wattn, qkva = slots.get((WATTN, part)), slots.get((QKVA, part))
            dqkv = b.dpre.at[part]

            def att_body(i, _, wattn=wattn):
                rows = at(i * 256, 256, 256)
                cols = slice(3 * part_cols, None)
                spans = [pl.ds(k * part_cols, part_cols) for k in range(4)]
                b.grad_att[rows, :] = sum(mm_cols(full[rows, s], wattn[s, cols]) for s in spans).astype(BF)
                return 0

            lax.fori_loop(0, length // 256, att_body, 0)
            lse_ref = r.lse.at[layer]
            attend_part_back(
                layer == 0,
                b.grad_att,
                qkva,
                lambda pair, rows, part=part, lse_ref=lse_ref: lse_ref[part, pair, :, rows],
                r.bias,
                dqkv,
                b.dk,
                b.dv,
                summing.advance,
            )
            n_full = slots.get(ROWS)

            def attn_chunk(i, rows, n_full=n_full, dqkv=dqkv, qkva=qkva):
                into_stage(i, mm_rows(n_full[:, rows], dqkv[:, : 3 * part_cols]), slice(0, 3 * part_cols))
                into_stage(i, mm_rows(qkva[:, 3 * part_cols :], full[:, rows]), slice(3 * part_cols, None))

            pending = store_chunks(o.foreign if part == 1 else o.own, base + 2, attn_chunk, pending)
        slots.drop((QKVA, 0), (QKVA, 1), ROWS)
        pending.wait()
        pending = None
        summing.ready = (base + 3) * per_matrix
        summing.feed()
        if layer == 1:
            slots.load((DOWN, 1), r.foreign_weights.at[0, 2])
            slots.load((SLOPE, 1), r.mats.at[0, 7])
            slots.load((ACT, 1), r.mats.at[0, 5])
        summing.advance()
        wattns = [slots.get((WATTN, 0)), slots.get((WATTN, 1))]

        def attn_partial(span, wattns=wattns):
            cols = slice(0, 3 * part_cols)
            return mm_cols(b.dpre[0, span, cols], wattns[0][:, cols]) + mm_cols(
                b.dpre[1, span, cols], wattns[1][:, cols]
            )

        scatter(turn + 1, attn_partial)
        slots.drop((WATTN, 0), (WATTN, 1))
        if layer == 1:
            slots.load(ROWS, r.mats.at[0, 3])
        norm_back(turn + 1, layer, 0, normed_copy, inverse_copy, layer == 0)
        if layer == 1:
            gather(turn + 2)
            summing.advance()

    other = at((1 - chip) * block, block, block)
    mine = at(chip * block, block, block)
    b.rows_send[...] = b.state[other, :].astype(BF)
    rows_copy = remote(b.rows_send, b.rows_recv, 16, {"tensor": flip(tensor, 2)})
    rows_copy.start()
    small = jnp.zeros(r.sel.shape[:1] + (width,), F32)
    for i in range(8):
        small = small + r.sel[:, i : i + 1] * vec[i : i + 1, :]
    b.small_buf[0, 0] = small

    def small_copy(i):
        return pltpu.make_async_remote_copy(
            src_ref=b.small_buf.at[0, i],
            dst_ref=b.small_buf.at[1, i],
            send_sem=b.small_send.at[i],
            recv_sem=b.small_recv.at[i],
            device_id=partners[i],
            device_id_type=MESH,
        )

    small_copy(0).start()
    for i in range(len(partners)):
        summing.advance()
        small_copy(i).wait()
        total = b.small_buf[0, i] + b.small_buf[1, i]
        if i + 1 < len(partners):
            b.small_buf[0, i + 1] = total
            small_copy(i + 1).start()
        else:
            o.small_out[...] = total
    rows_copy.wait()
    hidden_copy.wait()
    hidden_own_copy.wait()
    o.frames_grad[chip] = b.state[mine, :]
    o.frames_grad[1 - chip] = b.rows_recv[...].astype(F32)
    summing.drain()


ROWS, DOWN, SLOPE, ACT, UP, QKVA, WATTN, PACK = range(8)


class BackIn(NamedTuple):
    hidden: Any
    grad_in: Any
    mats: Any
    norms: Any
    inverses: Any
    foreign_weights: Any
    w_attn: Any
    w_up: Any
    w_down: Any
    gains: Any
    sel: Any
    bias: Any
    lse: Any


class BackOut(NamedTuple):
    down: Any
    up: Any
    attn: Any
    own: Any
    foreign: Any
    hidden_out: Any
    small_out: Any
    frames_grad: Any


class BackScratch(NamedTuple):
    slots: Any
    dpre: Any
    full: Any
    rs_send: Any
    rs_recv: Any
    state: Any
    keep: Any
    normed: Any
    inverse: Any
    stage: Any
    dk: Any
    dv: Any
    grad_att: Any
    vec: Any
    rows_send: Any
    rows_recv: Any
    small_buf: Any
    acc: Any
    seg: Any
    own_view: Any
    slot_sem: Any
    misc_sem: Any
    stage_sem: Any
    ex_send: Any
    ex_recv: Any
    small_send: Any
    small_recv: Any
    send_sem: Any
    recv_sem: Any
    copy_sem: Any
    view_sem: Any


def backward(inputs, size):
    half, width = inputs.grad_in.shape
    length = 2 * half
    block = length // 4
    bits = dp_bits(size)
    rows = 256
    matrices = 6
    chunks = matrices * length // rows
    stages = 2 * len(bits) + 1
    ring = min(chunks, max(2 * Summing.AHEAD + len(bits), 2 * len(bits)) + 1)
    steps = halvings(bits, rows, width)
    small_rows = inputs.sel.shape[0]
    exchanges = len(bits) + 2
    whole = jax.ShapeDtypeStruct((chunks, rows, width), BF)
    dma = pltpu.SemaphoreType.DMA
    shapes = BackScratch(
        slots=pltpu.VMEM((5, length, width), BF),
        dpre=pltpu.VMEM((2, length, width), BF),
        full=pltpu.VMEM((2, length, width), BF),
        rs_send=pltpu.VMEM((half, width), BF),
        rs_recv=pltpu.VMEM((2, half, width), BF),
        state=pltpu.VMEM((half, width), F32),
        keep=pltpu.VMEM((half, width), F32),
        normed=pltpu.VMEM((half, width), F32),
        inverse=pltpu.VMEM((half, LANES), F32),
        stage=pltpu.VMEM((length // rows, rows, width), BF),
        dk=pltpu.VMEM((length, LANES), F32),
        dv=pltpu.VMEM((length, LANES), F32),
        grad_att=pltpu.VMEM((length, width // 4), BF),
        vec=pltpu.VMEM((8, width), F32),
        rows_send=pltpu.VMEM((block, width), BF),
        rows_recv=pltpu.VMEM((block, width), BF),
        small_buf=pltpu.VMEM((2, exchanges, small_rows, width), F32),
        acc=pltpu.VMEM((ring, rows, width), BF),
        seg=pltpu.VMEM((chunks,) + steps[-1][:2], BF),
        own_view=pltpu.VMEM((2, rows, width), BF),
        slot_sem=dma((5,)),
        misc_sem=dma((4,)),
        stage_sem=dma((1,)),
        ex_send=dma((18,)),
        ex_recv=dma((18,)),
        small_send=dma((exchanges,)),
        small_recv=dma((exchanges,)),
        send_sem=dma((stages, chunks)),
        recv_sem=dma((stages, chunks)),
        copy_sem=dma((chunks,)),
        view_sem=dma((2,)),
    )
    scratch = list(shapes)
    scratch += [pltpu.VMEM((ring,) + step[:2], BF) for step in steps]
    any_spec = pl.BlockSpec(memory_space=pl.ANY)
    vmem_spec = pl.BlockSpec(memory_space=pltpu.VMEM)
    outs = pl.pallas_call(
        functools.partial(back_kernel, bits),
        in_specs=[any_spec] * 9 + [vmem_spec] * 4,
        out_specs=[any_spec] * 6 + [vmem_spec] * 2,
        out_shape=[jax.ShapeDtypeStruct((2, length // rows, rows, width), BF)] * 3
        + [whole] * 2
        + [
            jax.ShapeDtypeStruct((2, block, width), BF),
            jax.ShapeDtypeStruct((small_rows, width), F32),
            jax.ShapeDtypeStruct((2, block, width), F32),
        ],
        scratch_shapes=scratch,
        compiler_params=pltpu.CompilerParams(
            vmem_limit_bytes=VMEM_BYTES, collective_id=1, has_side_effects=True
        ),
        name="backward",
    )(*inputs)
    return BackOut(*outs)


class Fetching:
    SKEW = 2
    STAGES = 3

    def __init__(self, sources, targets, send_sem, recv_sem):
        self.sources, self.targets = sources, targets
        self.send_sem, self.recv_sem = send_sem, recv_sem
        self.dp = lax.axis_index("dp")
        self.tensor = lax.axis_index("tensor")
        self.half = sources[0].shape[0] // 2
        self.items = 2 * len(sources)
        self.step = 0

    def copies(self, stage, item):
        pieces = []
        for sub in range(2):
            first_bit = 1 + sub
            low = lax.rem(self.dp // first_bit, 2)
            high = lax.rem(self.dp // (3 - first_bit), 2)
            span = self.half // 2
            base = (item % 2) * self.half + sub * span
            quarter = span // 4
            if stage < 2:
                rows = at(base + (2 * high + low) * quarter, quarter, quarter)
            else:
                rows = at(base + high * 2 * quarter, 2 * quarter, 2 * quarter)
            target = self.targets[item // 2].at[rows]
            source = self.sources[item // 2].at[rows] if stage == 0 else target
            if stage == 0:
                device = {"tensor": flip(self.tensor, 2)}
            else:
                device = {"dp": flip(self.dp, first_bit if stage == 1 else 3 - first_bit)}
            pieces.append(
                pltpu.make_async_remote_copy(
                    src_ref=source,
                    dst_ref=target,
                    send_sem=self.send_sem.at[stage, item, sub],
                    recv_sem=self.recv_sem.at[stage, item, sub],
                    device_id=device,
                    device_id_type=MESH,
                )
            )
        return pieces

    def advance(self):
        step = self.step
        for stage in range(self.STAGES, 0, -1):
            item = step - self.SKEW * stage
            if 0 <= item < self.items:
                for copy in self.copies(stage - 1, item):
                    copy.wait_recv()
                if stage < self.STAGES:
                    for copy in self.copies(stage, item):
                        copy.start()
        if step < self.items:
            for copy in self.copies(0, step):
                copy.start()
        self.step += 1

    def need(self, matrix):
        while self.step <= 2 * matrix + 1 + self.SKEW * self.STAGES:
            self.advance()

    def drain(self):
        self.need(len(self.sources) - 1)
        for item in range(self.items):
            for stage in range(self.STAGES):
                for copy in self.copies(stage, item):
                    copy.wait_send()


def forward_kernel(bits, *refs):
    r, refs = ForwardIn(*refs[: len(ForwardIn._fields)]), refs[len(ForwardIn._fields) :]
    o, refs = ForwardOut(*refs[: len(ForwardOut._fields)]), refs[len(ForwardOut._fields) :]
    b = ForwardScratch(*refs)
    dp = lax.axis_index("dp")
    tensor = lax.axis_index("tensor")
    chip = tensor // 2
    core = lax.rem(tensor, 2)
    half, width = b.state.shape
    length = 2 * half
    block = length // 4
    part_cols = width // 4
    core_partner = {"tensor": flip(tensor, 1)}
    chip_partner = {"tensor": flip(tensor, 2)}
    partners = [core_partner, chip_partner] + [{"dp": flip(dp, bit)} for bit in bits[:2]]

    barrier = pltpu.get_barrier_semaphore()
    for partner in partners:
        pl.semaphore_signal(barrier, inc=1, device_id=partner, device_id_type=MESH)
    pl.semaphore_wait(barrier, len(partners))

    def remote(source, target, sem, device):
        return pltpu.make_async_remote_copy(
            src_ref=source,
            dst_ref=target,
            send_sem=b.ex_send.at[sem],
            recv_sem=b.ex_recv.at[sem],
            device_id=device,
            device_id_type=MESH,
        )

    def local(source, target, sem):
        return pltpu.make_async_copy(source, target, b.local_sem.at[sem])

    frames_copy = local(r.frames_got, b.frames_got, 3)
    frames_copy.start()
    own_copy = local(r.frames.at[chip], b.frames_own, 0)
    own_copy.start()

    slots = Slots(b.slots, b.slot_sem)

    def pack_copies(layer, slot):
        pairs = []
        for i in range(3):
            pairs.append((r.w_qkv.at[layer, i], slot.at[:, pl.ds(i * part_cols, part_cols)]))
        for k in range(4):
            span = pl.ds(k * part_cols, part_cols)
            pairs.append((r.w_out.at[layer, :, span], slot.at[span, pl.ds(3 * part_cols, part_cols)]))
        return [
            pltpu.make_async_copy(source, target, b.pack_sem.at[layer, i])
            for i, (source, target) in enumerate(pairs)
        ]

    pack_slots = [slots.reserve((WATTN, 0)), slots.reserve(PACK)]
    packs = [pack_copies(layer, slot) for layer, slot in enumerate(pack_slots)]
    stores = [
        pltpu.make_async_copy(slot, o.w_attn.at[layer], b.pack_sem.at[layer, 7])
        for layer, slot in enumerate(pack_slots)
    ]
    for pack in packs:
        for copy in pack:
            copy.start()
    for copy in packs[0]:
        copy.wait()
    stores[0].start()
    stores[0].wait()
    sources, targets = [], []
    for layer in range(2):
        sources += [o.w_attn.at[layer], r.w_up.at[layer], r.w_down.at[layer]]
        targets += [o.foreign_weights.at[layer, i] for i in range(3)]
    fetching = Fetching(sources, targets, b.send_sem, b.recv_sem)
    fetching.advance()
    fetching.advance()
    for copy in packs[1]:
        copy.wait()
    stores[1].start()
    own_copy.wait()
    frames_copy.wait()
    b.state[at(chip * block, block, block), :] = b.frames_own[...].astype(F32)
    b.state[at((1 - chip) * block, block, block), :] = b.frames_got[...].astype(F32)
    grad_copy = remote(r.out_grad.at[1 - chip], b.grad_got, 16, chip_partner)
    grad_own_copy = local(r.out_grad.at[chip], b.grad_own, 0)

    def exchange_copies(turn):
        full = b.full.at[turn % 2]
        spans = [at((2 * j + core) * block, block, block) for j in range(2)]
        return [remote(full.at[s], full.at[s], 4 * turn + j, core_partner) for j, s in enumerate(spans)]

    def scatter(turn, partial):
        copies = [
            remote(
                b.rs_send.at[pl.ds(j * block, block)],
                b.rs_recv.at[turn % 2, pl.ds(j * block, block)],
                4 * turn + 2 + j,
                core_partner,
            )
            for j in range(2)
        ]
        for j in range(2):
            span = at((2 * j + 1 - core) * block, block, block)
            b.rs_send[pl.ds(j * block, block), :] = partial(span).astype(BF)
            copies[j].start()
        for j in range(2):
            span = at((2 * j + core) * block, block, block)
            b.keep[pl.ds(j * block, block), :] = partial(span)
        for copy in copies:
            copy.wait()

    norm_copies = []

    def norm(turn, layer, which, add):
        for copy in norm_copies:
            copy.wait()
        norm_copies.clear()
        gain = r.gains[2 * layer + which : 2 * layer + which + 1, :]
        shift = r.shifts[2 * layer + which : 2 * layer + which + 1, :]
        step = 128
        copies = exchange_copies(turn)
        for j in range(2):

            def rows_body(i, _, j=j):
                span = at(j * block + i * step, step, step)
                state = b.state[span, :]
                if add:
                    state = state + (b.keep[span, :] + b.rs_recv[(turn - 1) % 2, span, :].astype(F32))
                    b.state[span, :] = state
                centred = state - jnp.mean(state, axis=-1, keepdims=True)
                variance = jnp.mean(centred * centred, axis=-1, keepdims=True)
                inverse = lax.rsqrt(variance + 1e-05)
                normed = centred * inverse
                b.normed[span, :] = normed
                b.inverse[span, :] = jnp.broadcast_to(inverse, (step, LANES))
                b.full[turn % 2, at((2 * j + core) * block + i * step, step, step), :] = (
                    normed * gain + shift
                ).astype(BF)
                return 0

            lax.fori_loop(0, block // step, rows_body, 0)
            copies[j].start()
        norm_copies.append(local(b.normed, o.norms.at[layer, which], 1))
        norm_copies.append(local(b.inverse, o.inverses.at[layer, which], 2))
        for copy in norm_copies:
            copy.start()
        for copy in copies:
            copy.wait()

    saves = []

    def save(source, target, sem):
        copy = local(source, target, sem)
        copy.start()
        saves.append(copy)

    def settle():
        for copy in saves:
            copy.wait()
        saves.clear()

    for layer in range(2):
        turn = 2 * layer
        norm(turn, layer, 0, layer == 1)
        if layer == 0:
            stores[1].wait()
            fetching.advance()
            fetching.advance()
        full = b.full.at[turn % 2]
        settle()
        save(full, o.mats.at[layer, 0], 3)
        fetching.advance()
        for part in range(2):
            if part == 1:
                fetching.need(3 * layer)
                slots.load((WATTN, 1), o.foreign_weights.at[layer, 0])
            calls = [layer == 0 and part == 1]

            def steps(calls=calls):
                if calls:
                    skip = calls.pop()
                    if skip:
                        return
                fetching.advance()

            attend_part(
                layer == 0, full, slots.get((WATTN, part)), r.bias, b.acts.at[part], o.lse.at[layer, part], steps
            )
            save(b.acts.at[part], o.mats.at[layer, 1 + part], 4 + part)
            if part == 0:
                slots.load((UP, 0), r.w_up.at[layer])
                slots.load((DOWN, 0), r.w_down.at[layer])
        weights = [slots.get((WATTN, part)) for part in range(2)]

        def out_partial(span, weights=weights):
            cols = slice(3 * part_cols, None)
            first, second = b.acts[0, span, cols], b.acts[1, span, cols]
            spans = [pl.ds(k * part_cols, part_cols) for k in range(4)]
            return jnp.concatenate(
                [mm(first, weights[0][s, cols]) + mm(second, weights[1][s, cols]) for s in spans], axis=1
            )

        scatter(turn, out_partial)
        slots.drop((WATTN, 0), (WATTN, 1))
        fetching.advance()
        turn += 1
        norm(turn, layer, 1, True)
        full = b.full.at[turn % 2]
        settle()
        save(full, o.mats.at[layer, 3], 3)
        for part in range(2):
            if part == 1:
                fetching.need(3 * layer + 1)
                slots.load((UP, 1), o.foreign_weights.at[layer, 1])
            up = slots.get((UP, part))

            def up_body(i, _, part=part, up=up, full=full):
                rows = at(i * 256, 256, 256)
                for first in range(0, width, 256):
                    cols = pl.ds(first, 256)
                    active, slope = gelu_parts(mm(full[rows, :], up[:, cols]))
                    b.acts[part, rows, cols] = active.astype(BF)
                    b.slope[part, rows, cols] = slope.astype(BF)
                return 0

            lax.fori_loop(0, length // 256, up_body, 0)
            save(b.acts.at[part], o.mats.at[layer, 4 + part], 4 + part)
            save(b.slope.at[part], o.mats.at[layer, 6 + part], 6 + part)
            slots.drop((UP, part))
        fetching.need(3 * layer + 2)
        slots.load((DOWN, 1), o.foreign_weights.at[layer, 2])
        downs = [slots.get((DOWN, part)) for part in range(2)]

        def down_partial(span, downs=downs):
            return mm(b.acts[0, span, :], downs[0][...]) + mm(b.acts[1, span, :], downs[1][...])

        scatter(turn, down_partial)
        slots.drop((DOWN, 0), (DOWN, 1))
        if layer == 0:
            slots.rename(PACK, (WATTN, 0))
            grad_copy.start()
            grad_own_copy.start()

    for j in range(2):
        span = pl.ds(j * block, block)
        total = b.state[span, :] + (b.keep[span, :] + b.rs_recv[1, span, :].astype(F32))
        o.hidden[j] = total.astype(BF)
    grad_own_copy.wait()
    grad_copy.wait()
    o.grad_in[at(chip * block, block, block), :] = b.grad_own[...].astype(F32)
    o.grad_in[at((1 - chip) * block, block, block), :] = b.grad_got[...].astype(F32)
    fetching.drain()
    settle()
    for copy in norm_copies:
        copy.wait()


class ForwardIn(NamedTuple):
    frames: Any
    frames_got: Any
    out_grad: Any
    w_qkv: Any
    w_out: Any
    w_up: Any
    w_down: Any
    gains: Any
    shifts: Any
    bias: Any


class ForwardOut(NamedTuple):
    mats: Any
    norms: Any
    inverses: Any
    foreign_weights: Any
    w_attn: Any
    lse: Any
    grad_in: Any
    hidden: Any


class ForwardScratch(NamedTuple):
    slots: Any
    acts: Any
    slope: Any
    full: Any
    rs_send: Any
    rs_recv: Any
    state: Any
    keep: Any
    normed: Any
    inverse: Any
    frames_own: Any
    frames_got: Any
    grad_own: Any
    grad_got: Any
    slot_sem: Any
    local_sem: Any
    pack_sem: Any
    ex_send: Any
    ex_recv: Any
    send_sem: Any
    recv_sem: Any


def forward(inputs, size):
    block, width = inputs.frames.shape[1:]
    half, length = 2 * block, 4 * block
    bits = dp_bits(size)
    dma = pltpu.SemaphoreType.DMA
    rows = pltpu.VMEM((block, width), BF)
    scratch = ForwardScratch(
        slots=pltpu.VMEM((5, length, width), BF),
        acts=pltpu.VMEM((2, length, width), BF),
        slope=pltpu.VMEM((2, length, width), BF),
        full=pltpu.VMEM((2, length, width), BF),
        rs_send=pltpu.VMEM((half, width), BF),
        rs_recv=pltpu.VMEM((2, half, width), BF),
        state=pltpu.VMEM((half, width), F32),
        keep=pltpu.VMEM((half, width), F32),
        normed=pltpu.VMEM((half, width), F32),
        inverse=pltpu.VMEM((half, LANES), F32),
        frames_own=rows,
        frames_got=rows,
        grad_own=rows,
        grad_got=rows,
        slot_sem=dma((5,)),
        local_sem=dma((8,)),
        pack_sem=dma((2, 8)),
        ex_send=dma((17,)),
        ex_recv=dma((17,)),
        send_sem=dma((3, 12, 2)),
        recv_sem=dma((3, 12, 2)),
    )
    out_shape = ForwardOut(
        mats=jax.ShapeDtypeStruct((2, 8, length, width), BF),
        norms=jax.ShapeDtypeStruct((2, 2, half, width), F32),
        inverses=jax.ShapeDtypeStruct((2, 2, half, LANES), F32),
        foreign_weights=jax.ShapeDtypeStruct((2, 3, length, width), BF),
        w_attn=jax.ShapeDtypeStruct((2, length, width), BF),
        lse=jax.ShapeDtypeStruct((2, 2, width // (4 * LANES), 8, length), F32),
        grad_in=jax.ShapeDtypeStruct((half, width), F32),
        hidden=jax.ShapeDtypeStruct((2, block, width), BF),
    )
    any_spec = pl.BlockSpec(memory_space=pl.ANY)
    vmem_spec = pl.BlockSpec(memory_space=pltpu.VMEM)
    outs = pl.pallas_call(
        functools.partial(forward_kernel, bits),
        in_specs=[any_spec] * 7 + [vmem_spec] * 3,
        out_specs=[any_spec] * 5 + [vmem_spec] * 3,
        out_shape=list(out_shape),
        scratch_shapes=list(scratch),
        compiler_params=pltpu.CompilerParams(
            vmem_limit_bytes=VMEM_BYTES, collective_id=2, has_side_effects=True
        ),
        name="forward",
    )(*inputs)
    return ForwardOut(*outs)


def per_device(
    frames, lengths, codebook, ln_gain, ln_bias, ada_scale, ada_shift, w_qkv, w_out, w_up, w_down, out_grad
):
    chip = lax.axis_index("tensor") // 2
    length = frames.shape[1] * lax.axis_size("tensor")
    size = lax.axis_size("dp")

    def pick(pair):
        return jnp.where(chip == 0, pair[0], pair[1])

    bias = jnp.where(jnp.arange(length) < pick(lengths), 0.0, -1e30).astype(F32)
    sections = ada_scale.shape[0]
    chosen = (jnp.arange(sections) == pick(codebook))[:, None, None]
    gains = jnp.concatenate([ln_gain, jnp.sum(jnp.where(chosen, ada_scale, 0.0), axis=0)])
    shifts = jnp.concatenate([ln_bias, jnp.sum(jnp.where(chosen, ada_shift, 0.0), axis=0)])
    pairs = [(i, i ^ 2) for i in range(lax.axis_size("tensor"))]
    frames_got = lax.ppermute(jnp.where(chip == 0, frames[1], frames[0]), "tensor", pairs)
    w_by_kind = w_qkv.transpose(0, 2, 1, 3)
    ahead = forward(
        ForwardIn(
            frames, frames_got, out_grad, w_by_kind, w_out, w_up, w_down, gains, shifts, bias[None, :]
        ),
        size,
    )
    unit = jnp.eye(8, dtype=F32)
    sel = jnp.concatenate(
        [unit[0:3:2], unit[1:4:2]]
        + [jnp.where(chosen, rows[None], 0.0).reshape(2 * sections, 8) for rows in (unit[4:7:2], unit[5:8:2])]
    )
    back = backward(
        BackIn(
            ahead.hidden,
            ahead.grad_in,
            ahead.mats,
            ahead.norms,
            ahead.inverses,
            ahead.foreign_weights,
            ahead.w_attn,
            w_up,
            w_down,
            gains,
            sel,
            bias[:, None],
            ahead.lse,
        ),
        size,
    )
    small = back.small_out
    layers, part, width = w_out.shape
    attn = back.attn.reshape(layers, width, width)
    grad_qkv = jnp.stack([attn[:, :, i * part : (i + 1) * part].astype(F32) for i in range(3)], axis=1)
    quarters = [back.attn[:, k, :, 3 * part :].astype(F32) for k in range(width // part)]
    grad_out = jnp.concatenate(quarters, axis=2)
    return (
        back.hidden_out,
        back.frames_grad,
        small[0:2],
        small[2:4],
        small[4 : 4 + 2 * sections].reshape(ada_scale.shape),
        small[4 + 2 * sections :].reshape(ada_scale.shape),
        grad_qkv.transpose(0, 2, 1, 3),
        grad_out.reshape(w_out.shape),
        back.up.astype(F32).reshape(w_up.shape),
        back.down.astype(F32).reshape(w_down.shape),
    )


def solution(mesh):
    placed = (
        P("dp", "tensor", None),
        P("dp"),
        P("dp"),
        P(),
        P(),
        P(),
        P(),
        P(None, None, None, "tensor"),
        P(None, "tensor", None),
        P(None, None, "tensor"),
        P(None, "tensor", None),
        P("dp", "tensor", None),
    )
    return jax.shard_map(
        per_device,
        mesh=mesh,
        in_specs=placed,
        out_specs=(
            P("dp", "tensor", None),
            P("dp", "tensor", None),
            P(),
            P(),
            P(),
            P(),
            P(None, None, None, "tensor"),
            P(None, "tensor", None),
            P(None, None, "tensor"),
            P(None, "tensor", None),
        ),
        check_vma=False,
    )
```

```python
import functools
from typing import Any, NamedTuple

import jax
import jax.numpy as jnp
from jax import lax
from jax.experimental import pallas as pl
from jax.experimental.pallas import tpu as pltpu
from jax.sharding import PartitionSpec as P

HEAD_DIM = 64
BF = jnp.bfloat16
F32 = jnp.float32
HIGH = lax.Precision.HIGHEST
MESH = pl.DeviceIdType.MESH
VMEM_BYTES = 60 << 20
LANES = 128


def mm(left, right):
    return jnp.dot(left, right, preferred_element_type=F32)


def mm_rows(left, right):
    return lax.dot_general(left, right, (((0,), (0,)), ((), ())), preferred_element_type=F32)


def mm_cols(left, right, precision=None):
    return lax.dot_general(
        left, right, (((1,), (1,)), ((), ())), precision=precision, preferred_element_type=F32
    )


def head_of_lane(shape):
    return lax.broadcasted_iota(jnp.int32, shape, len(shape) - 1) // HEAD_DIM


def at(start, size, unit):
    return pl.ds(pl.multiple_of(start, unit), size)


def flip(index, bit):
    return index + bit - 2 * bit * lax.rem(index // bit, 2)


def dp_bits(size):
    bits = []
    while 2 ** len(bits) < size:
        bits.append(2 ** len(bits))
    return bits


def own_rows_first(body, arrive):
    core = lax.rem(lax.axis_index("tensor"), 2)

    def own_body(j, _):
        body(2 * j + core)
        return 0

    def other_body(j, _):
        body(2 * j + 1 - core)
        return 0

    lax.fori_loop(0, 2, own_body, 0)
    arrive()
    lax.fori_loop(0, 2, other_body, 0)


def attend_part(causal, n_ref, w_ref, bias_ref, qkva_ref, lse_ref, arrive, between):
    length = n_ref.shape[0]
    part = qkva_ref.shape[1] // 4
    block = length // 4
    scaling = HEAD_DIM ** (-0.5)

    def project(index):
        rows = at(index * block, block, block)
        qkva_ref[rows, : 3 * part] = mm(n_ref[rows, :], w_ref[:, : 3 * part]).astype(BF)

    own_rows_first(project, arrive)

    for pair in range(part // LANES):
        q_cols, k_cols, v_cols, a_cols = [pl.ds(i * part + pair * LANES, LANES) for i in range(4)]
        for first in range(0, length, block):
            rows = pl.ds(first, block)
            reach = first + block if causal else length
            queries = qkva_ref[rows, q_cols] * jnp.asarray(scaling, BF)
            keys = qkva_ref[pl.ds(0, reach), k_cols]
            values = qkva_ref[pl.ds(0, reach), v_cols]
            bias = bias_ref[:, pl.ds(0, reach)]
            head = head_of_lane(queries.shape)
            lanes = lax.broadcasted_iota(jnp.int32, (block, LANES), 1)
            mixed = None
            stats = jnp.zeros((block, LANES), F32)
            for which in range(2):
                scores = mm_cols(jnp.where(head == which, queries, jnp.zeros_like(queries)), keys) + bias
                if causal:
                    query_at = lax.broadcasted_iota(jnp.int32, (block, block), 0)
                    key_at = lax.broadcasted_iota(jnp.int32, (block, block), 1)
                    last = jnp.where(key_at <= query_at, scores[:, first:], -1e30)
                    scores = jnp.concatenate([scores[:, :first], last], axis=1) if first else last
                row_max = jnp.max(scores, axis=-1, keepdims=True)
                raised = jnp.exp(scores - row_max)
                total = jnp.sum(raised, axis=-1, keepdims=True)
                one = mm(raised.astype(BF), values) * (1.0 / total)
                mixed = one if mixed is None else jnp.where(head == 0, mixed, one)
                stats = jnp.where(lanes == which, row_max + jnp.log(total), stats)
            qkva_ref[rows, a_cols] = mixed.astype(BF)
            square = lax.broadcasted_iota(jnp.int32, (8, LANES), 1)
            pick = (square == lax.broadcasted_iota(jnp.int32, (8, LANES), 0)).astype(F32)
            lse_ref[pair, :, rows] = mm_cols(pick, stats, HIGH)
        between()


def attend_part_back(causal, grad_att_ref, qkva_ref, lse_of, bias_ref, dqkv_ref, dk_ref, dv_ref, between):
    length = qkva_ref.shape[0]
    part = qkva_ref.shape[1] // 4
    block = length // 4
    scaling = HEAD_DIM ** (-0.5)

    for pair in range(part // LANES):
        q_cols, k_cols, v_cols, a_cols = [pl.ds(i * part + pair * LANES, LANES) for i in range(4)]
        g_cols = pl.ds(pair * LANES, LANES)
        dk_ref[...] = jnp.zeros_like(dk_ref)
        dv_ref[...] = jnp.zeros_like(dv_ref)
        keys_turned = qkva_ref[:, k_cols].astype(F32).T.astype(BF)
        feature = lax.broadcasted_iota(jnp.int32, keys_turned.shape, 0) // HEAD_DIM
        turned = [
            jnp.where(feature == which, keys_turned, jnp.zeros_like(keys_turned)) for which in range(2)
        ]
        for first in range(0, length, block):
            rows = pl.ds(first, block)
            reach = first + block if causal else length
            queries = qkva_ref[rows, q_cols] * jnp.asarray(scaling, BF)
            grads = grad_att_ref[rows, g_cols]
            head = head_of_lane(queries.shape)
            pick = (head_of_lane((8, LANES)) == lax.broadcasted_iota(jnp.int32, (8, LANES), 0)).astype(F32)
            product = grads.astype(F32) * qkva_ref[rows, a_cols].astype(F32)
            delta = mm_cols(pick, product, HIGH)
            lse = lse_of(pair, rows)
            keys = qkva_ref[pl.ds(0, reach), k_cols]
            values = qkva_ref[pl.ds(0, reach), v_cols]
            bias = bias_ref[pl.ds(0, reach), :]
            dq_turned = None
            for which in range(2):
                queries_one = jnp.where(head == which, queries, jnp.zeros_like(queries))
                grads_one = jnp.where(head == which, grads, jnp.zeros_like(grads))
                scores = mm_cols(keys, queries_one) + bias
                if causal:
                    key_at = lax.broadcasted_iota(jnp.int32, (block, block), 0)
                    query_at = lax.broadcasted_iota(jnp.int32, (block, block), 1)
                    last = jnp.where(key_at <= query_at, scores[first:], -1e30)
                    scores = jnp.concatenate([scores[:first], last], axis=0) if first else last
                probs = jnp.exp(scores - lse[which : which + 1])
                grad_probs = mm_cols(values, grads_one)
                grad_scores = (probs * (grad_probs - delta[which : which + 1])).astype(BF)
                dv_ref[pl.ds(0, reach), :] += mm(probs.astype(BF), grads_one)
                dk_ref[pl.ds(0, reach), :] += mm(grad_scores, queries_one)
                one = mm(turned[which][:, :reach], grad_scores)
                dq_turned = one if dq_turned is None else dq_turned + one
            dqkv_ref[rows, q_cols] = (dq_turned.T * scaling).astype(BF)
        dqkv_ref[:, k_cols] = dk_ref[...].astype(BF)
        dqkv_ref[:, v_cols] = dv_ref[...].astype(BF)
        between()


def gelu_parts(hidden):
    bell = jnp.exp(-0.5 * hidden * hidden)
    base = 1.0 + 0.23164189 * jnp.abs(hidden)
    t = pl.reciprocal(base, approx=True)
    t = t * (2.0 - base * t)
    poly = 0.5307027145
    poly = poly * t - 0.7265760135
    poly = poly * t + 0.7107068705
    poly = poly * t - 0.142248368
    poly = poly * t + 0.127414796
    tail = poly * t * bell
    cdf = jnp.where(hidden >= 0, 1.0 - tail, tail)
    return hidden * cdf, cdf + hidden * bell * 0.3989422804014327


class Slots:
    def __init__(self, buffers, sems):
        self.buffers = buffers
        self.sems = sems
        self.free = list(range(buffers.shape[0]))
        self.held = {}

    def load(self, name, source):
        slot = self.free.pop(0)
        copy = pltpu.make_async_copy(source, self.buffers.at[slot], self.sems.at[slot])
        copy.start()
        self.held[name] = [slot, copy]

    def get(self, name):
        slot, copy = self.held[name]
        if copy is not None:
            copy.wait()
            self.held[name][1] = None
        return self.buffers.at[slot]

    def reserve(self, name):
        slot = self.free.pop(0)
        self.held[name] = [slot, None]
        return self.buffers.at[slot]

    def rename(self, old, new):
        self.held[new] = self.held.pop(old)

    def drop(self, *names):
        for name in names:
            self.free.append(self.held.pop(name)[0])


class Summing:
    AHEAD = 4

    def __init__(self, bits, own, foreign, outs, acc, seg, own_view, rbufs, send_sem, recv_sem, copy_sem, view_sem):
        self.bits, self.own, self.foreign, self.outs = bits, own, foreign, outs
        self.acc, self.seg, self.own_view, self.rbufs = acc, seg, own_view, rbufs
        self.send_sem, self.recv_sem, self.copy_sem, self.view_sem = send_sem, recv_sem, copy_sem, view_sem
        self.chunks, self.rows, self.columns = own.shape
        self.ring = acc.shape[0]
        self.stages = 2 * len(bits) + 1
        self.dp = lax.axis_index("dp")
        self.tensor = lax.axis_index("tensor")
        self.step = 0
        self.started = 0
        self.ready = 0
        self.sizes = [step[:2] for step in halvings(bits, self.rows, self.columns)]
        row, column = 0, 0
        self.plan = []
        for half_rows, half_columns, bit, by_rows in halvings(bits, self.rows, self.columns):
            flag = lax.rem(self.dp // bit, 2)
            if by_rows:
                keep = (row + flag * half_rows, column)
                send = (row + (1 - flag) * half_rows, column)
            else:
                keep = (row, column + flag * half_columns)
                send = (row, column + (1 - flag) * half_columns)
            row, column = keep
            self.plan.append((keep, send, bit))

    def region(self, where, size):
        return at(where[0], size[0], 16), at(where[1], size[1], LANES)

    def place(self, c):
        per_matrix = self.outs[0].shape[1]
        matrix = c // per_matrix
        return self.outs[matrix % 3].at[1 - matrix // 3, c % per_matrix]

    def copy(self, s, c):
        count = len(self.bits)
        slot = c % self.ring
        if s == 0:
            source, target = self.foreign.at[c], self.acc.at[slot]
            device = {"tensor": flip(self.tensor, 2)}
        elif s <= count:
            i = s - 1
            _, send, bit = self.plan[i]
            rows, columns = self.region(send, self.sizes[i])
            source = self.acc.at[slot, rows, columns]
            target, device = self.rbufs[i].at[slot], {"dp": flip(self.dp, bit)}
        else:
            i = 2 * count - s
            keep, _, bit = self.plan[i]
            rows, columns = self.region(keep, self.sizes[i])
            target = self.place(c).at[rows, columns]
            source = self.seg.at[c] if i == count - 1 else target
            device = {"dp": flip(self.dp, bit)}
        return pltpu.make_async_remote_copy(
            src_ref=source,
            dst_ref=target,
            send_sem=self.send_sem.at[s, c],
            recv_sem=self.recv_sem.at[s, c],
            device_id=device,
            device_id_type=MESH,
        )

    def seg_copy(self, c):
        rows, columns = self.region(self.plan[-1][0], self.sizes[-1])
        return pltpu.make_async_copy(self.seg.at[c], self.place(c).at[rows, columns], self.copy_sem.at[c])

    def view(self, c):
        return pltpu.make_async_copy(self.own.at[c], self.own_view.at[c % 2], self.view_sem.at[c % 2])

    def finish(self, s, c):
        count = len(self.bits)
        slot = c % self.ring
        self.copy(s, c).wait_recv()
        if s == 0:
            self.view(c).wait()
            self.acc[slot] = (self.own_view[c % 2].astype(F32) + self.acc[slot].astype(F32)).astype(BF)
        elif s <= count:
            i = s - 1
            rows, columns = self.region(self.plan[i][0], self.sizes[i])
            total = self.acc[slot, rows, columns].astype(F32) + self.rbufs[i][slot].astype(F32)
            if s == count:
                self.seg[c] = total.astype(BF)
                self.seg_copy(c).start()
                for stage in range(1, count + 1):
                    self.copy(stage, c).wait_send()
            else:
                self.acc[slot, rows, columns] = total.astype(BF)
        elif s == count + 1:
            self.seg_copy(c).wait()

    def advance(self):
        step = self.step
        if step < self.chunks:
            self.view(step).start()
        for s in range(self.stages - 1, -1, -1):
            c = step - s
            if 0 <= c < self.chunks:
                self.finish(s, c)
                if s + 1 < self.stages:
                    self.copy(s + 1, c).start()
        self.step += 1
        self.feed()

    def feed(self):
        ahead = self.AHEAD if self.step < self.chunks // 2 else 2
        while self.started < min(self.ready, self.step + ahead):
            self.copy(0, self.started).start()
            self.started += 1

    def drain(self):
        while self.step < self.chunks + self.stages - 1:
            self.advance()
        count = len(self.bits)
        for c in range(self.chunks):
            for s in range(self.stages):
                if not 1 <= s <= count:
                    self.copy(s, c).wait_send()


def halvings(bits, rows, columns):
    steps = []
    for bit in bits:
        by_rows = rows >= 32
        rows, columns = (rows // 2, columns) if by_rows else (rows, columns // 2)
        steps.append((rows, columns, bit, by_rows))
    return steps


def back_kernel(bits, *refs):
    r, refs = BackIn(*refs[: len(BackIn._fields)]), refs[len(BackIn._fields) :]
    o, refs = BackOut(*refs[: len(BackOut._fields)]), refs[len(BackOut._fields) :]
    b, rbufs = BackScratch(*refs[: len(BackScratch._fields)]), refs[len(BackScratch._fields) :]
    dp = lax.axis_index("dp")
    tensor = lax.axis_index("tensor")
    chip = tensor // 2
    core = lax.rem(tensor, 2)
    half, width = b.state.shape
    length = 2 * half
    block = length // 4
    core_partner = {"tensor": flip(tensor, 1)}
    partners = [core_partner, {"tensor": flip(tensor, 2)}] + [{"dp": flip(dp, bit)} for bit in bits]

    barrier = pltpu.get_barrier_semaphore()
    for partner in partners:
        pl.semaphore_signal(barrier, inc=1, device_id=partner, device_id_type=MESH)
    pl.semaphore_wait(barrier, len(partners))

    slots = Slots(b.slots, b.slot_sem)
    summing = Summing(
        bits, o.own, o.foreign, (o.down, o.up, o.attn), b.acc, b.seg, b.own_view,
        rbufs, b.send_sem, b.recv_sem, b.copy_sem, b.view_sem,
    )
    per_matrix = length // summing.rows
    vec = b.vec
    vec[...] = jnp.zeros_like(vec)
    section = r.codebook[chip]
    choose_maps(b.gains, r.ln_gain, r.ada_scale, section)
    key_at = lax.broadcasted_iota(jnp.int32, (length, 1), 0)
    b.bias[...] = jnp.where(key_at < r.lengths[chip], 0.0, -1e30).astype(F32)

    def remote(source, target, sem, device):
        return pltpu.make_async_remote_copy(
            src_ref=source,
            dst_ref=target,
            send_sem=b.ex_send.at[sem],
            recv_sem=b.ex_recv.at[sem],
            device_id=device,
            device_id_type=MESH,
        )

    def exchange_copies(turn):
        full = b.full.at[turn % 2]
        spans = [at((2 * j + core) * block, block, block) for j in range(2)]
        return [remote(full.at[s], full.at[s], 4 * turn + j, core_partner) for j, s in enumerate(spans)]

    def exchange_start(turn, j):
        exchange_copies(turn)[j].start()

    def exchange_wait(turn):
        for copy in exchange_copies(turn):
            copy.wait()

    def scatter_copies(turn):
        return [
            remote(
                b.rs_send.at[pl.ds(j * block, block)],
                b.rs_recv.at[turn % 2, pl.ds(j * block, block)],
                4 * turn + 2 + j,
                core_partner,
            )
            for j in range(2)
        ]

    def scatter(turn, partial):
        copies = scatter_copies(turn)
        for j in range(2):
            span = at((2 * j + 1 - core) * block, block, block)
            b.rs_send[pl.ds(j * block, block), :] = partial(span).astype(BF)
            copies[j].start()
        for j in range(2):
            span = at((2 * j + core) * block, block, block)
            b.keep[pl.ds(j * block, block), :] = partial(span)
        for copy in copies:
            copy.wait()

    def norm_back(turn, layer, which, normed_copy, inverse_copy, last):
        normed_copy.wait()
        inverse_copy.wait()
        index = 4 * layer + 2 * which
        gain = b.gains[2 * layer + which : 2 * layer + which + 1, :]
        step = 128

        def rows_body(i, _):
            span = at(i * step, step, step)
            grad = b.keep[span, :] + b.rs_recv[turn % 2, span, :].astype(F32)
            normed = b.normed[span, :]
            moved = grad * gain
            mean_grad = jnp.mean(moved, axis=-1, keepdims=True)
            mean_proj = jnp.mean(moved * normed, axis=-1, keepdims=True)
            state = b.state[span, :] + b.inverse[span, :1] * (moved - mean_grad - normed * mean_proj)
            b.state[span, :] = state
            vec[index : index + 1, :] += jnp.sum(grad * normed, axis=0, keepdims=True)
            vec[index + 1 : index + 2, :] += jnp.sum(grad, axis=0, keepdims=True)
            return 0

        lax.fori_loop(0, half // step, rows_body, 0)

    def gather(turn):
        for j in range(2):
            span = at((2 * j + core) * block, block, block)
            b.full[turn % 2, span, :] = b.state[pl.ds(j * block, block), :].astype(BF)
            exchange_start(turn, j)

    def store_chunks(where, matrix, chunk_of, previous):
        if previous is not None:
            previous.wait()
        stage = b.stage

        def body(i, _):
            chunk_of(i, at(i * summing.rows, summing.rows, summing.rows))
            return 0

        lax.fori_loop(0, per_matrix, body, 0)
        copy = pltpu.make_async_copy(
            stage, where.at[pl.ds(matrix * per_matrix, per_matrix)], b.stage_sem.at[0]
        )
        copy.start()
        return copy

    def into_stage(i, value, columns=slice(None)):
        b.stage[i, :, columns] = value.astype(BF)

    hidden_copy = remote(r.hidden.at[1 - chip], o.hidden_out.at[chip], 17, {"tensor": flip(tensor, 2)})
    hidden_copy.start()
    hidden_own_copy = pltpu.make_async_copy(r.hidden.at[chip], o.hidden_out.at[chip], b.misc_sem.at[3])
    hidden_own_copy.start()
    state_copy = pltpu.make_async_copy(r.grad_in, b.state, b.misc_sem.at[0])
    state_copy.start()
    slots.load((DOWN, 1), r.foreign_weights.at[1, 2])
    slots.load((SLOPE, 1), r.mats.at[1, 7])
    slots.load((ACT, 1), r.mats.at[1, 5])
    slots.load(ROWS, r.mats.at[1, 3])
    state_copy.wait()
    gather(0)
    pending = None

    for layer in (1, 0):
        base = 0 if layer == 1 else 3
        turn = 0 if layer == 1 else 2
        exchange_wait(turn)
        full = b.full.at[turn % 2]
        normed_copy = pltpu.make_async_copy(r.norms.at[layer, 1], b.normed, b.misc_sem.at[1])
        normed_copy.start()
        inverse_copy = pltpu.make_async_copy(r.inverses.at[layer, 1], b.inverse, b.misc_sem.at[2])
        inverse_copy.start()
        for part in (1, 0):
            where = o.foreign if part == 1 else o.own
            act, n_full = slots.get((ACT, part)), slots.get(ROWS)
            dpre = b.dpre.at[part]

            def down_chunk(i, rows, act=act):
                into_stage(i, mm_rows(act[:, rows], full[...]))

            def up_chunk(i, rows, n_full=n_full, dpre=dpre):
                into_stage(i, mm_rows(n_full[:, rows], dpre[...]))

            pending = store_chunks(where, base, down_chunk, pending)
            slots.drop((ACT, part))
            if part == 1:
                slots.load((ACT, 0), r.mats.at[layer, 4])
            else:
                slots.load((UP, 1), r.foreign_weights.at[layer, 1])
            down, slope = slots.get((DOWN, part)), slots.get((SLOPE, part))

            def slope_body(i, _, down=down, slope=slope, dpre=dpre):
                rows = at(i * 256, 256, 256)
                dpre[rows, :] = (mm_cols(full[rows, :], down[...]) * slope[rows, :].astype(F32)).astype(BF)
                return 0

            if part == 1:
                pending.wait()
                pending = None
                summing.ready = (base + 1) * per_matrix
                summing.feed()
            lax.fori_loop(0, length // 256, slope_body, 0)
            slots.drop((DOWN, part), (SLOPE, part))
            if part == 1:
                slots.load((DOWN, 0), r.w_down.at[layer])
                slots.load((SLOPE, 0), r.mats.at[layer, 6])
            else:
                slots.load((UP, 0), r.w_up.at[layer])
            pending = store_chunks(where, base + 1, up_chunk, pending)
            if part == 1:
                pending.wait()
                pending = None
                summing.ready = (base + 2) * per_matrix
                summing.feed()
            if layer == 0:
                summing.advance()
        slots.drop(ROWS)
        pending.wait()
        pending = None
        summing.advance()
        ups = [slots.get((UP, 0)), slots.get((UP, 1))]

        def up_partial(span, ups=ups):
            return mm_cols(b.dpre[0, span, :], ups[0][...]) + mm_cols(b.dpre[1, span, :], ups[1][...])

        scatter(turn, up_partial)
        slots.drop((UP, 0), (UP, 1))
        slots.load((QKVA, 1), r.mats.at[layer, 2])
        slots.load((WATTN, 1), r.foreign_weights.at[layer, 0])
        slots.load(ROWS, r.mats.at[layer, 0])
        slots.load((QKVA, 0), r.mats.at[layer, 1])
        slots.load((WATTN, 0), r.w_attn.at[layer])
        norm_back(turn, layer, 1, normed_copy, inverse_copy, False)
        gather(turn + 1)
        summing.advance()
        normed_copy = pltpu.make_async_copy(r.norms.at[layer, 0], b.normed, b.misc_sem.at[1])
        normed_copy.start()
        inverse_copy = pltpu.make_async_copy(r.inverses.at[layer, 0], b.inverse, b.misc_sem.at[2])
        inverse_copy.start()
        exchange_wait(turn + 1)
        full = b.full.at[(turn + 1) % 2]
        part_cols = width // 4
        for part in (1, 0):
            wattn, qkva = slots.get((WATTN, part)), slots.get((QKVA, part))
            dqkv = b.dpre.at[part]

            def att_body(i, _, wattn=wattn):
                rows = at(i * 256, 256, 256)
                cols = slice(3 * part_cols, None)
                spans = [pl.ds(k * part_cols, part_cols) for k in range(4)]
                b.grad_att[rows, :] = sum(mm_cols(full[rows, s], wattn[s, cols]) for s in spans).astype(BF)
                return 0

            lax.fori_loop(0, length // 256, att_body, 0)
            lse_ref = r.lse.at[layer]
            attend_part_back(
                layer == 0,
                b.grad_att,
                qkva,
                lambda pair, rows, part=part, lse_ref=lse_ref: lse_ref[part, pair, :, rows],
                b.bias,
                dqkv,
                b.dk,
                b.dv,
                summing.advance,
            )
            n_full = slots.get(ROWS)

            def attn_chunk(i, rows, n_full=n_full, dqkv=dqkv, qkva=qkva):
                into_stage(i, mm_rows(n_full[:, rows], dqkv[:, : 3 * part_cols]), slice(0, 3 * part_cols))
                into_stage(i, mm_rows(qkva[:, 3 * part_cols :], full[:, rows]), slice(3 * part_cols, None))

            pending = store_chunks(o.foreign if part == 1 else o.own, base + 2, attn_chunk, pending)
        slots.drop((QKVA, 0), (QKVA, 1), ROWS)
        pending.wait()
        pending = None
        summing.ready = (base + 3) * per_matrix
        summing.feed()
        if layer == 1:
            slots.load((DOWN, 1), r.foreign_weights.at[0, 2])
            slots.load((SLOPE, 1), r.mats.at[0, 7])
            slots.load((ACT, 1), r.mats.at[0, 5])
        summing.advance()
        wattns = [slots.get((WATTN, 0)), slots.get((WATTN, 1))]

        def attn_partial(span, wattns=wattns):
            cols = slice(0, 3 * part_cols)
            return mm_cols(b.dpre[0, span, cols], wattns[0][:, cols]) + mm_cols(
                b.dpre[1, span, cols], wattns[1][:, cols]
            )

        scatter(turn + 1, attn_partial)
        slots.drop((WATTN, 0), (WATTN, 1))
        if layer == 1:
            slots.load(ROWS, r.mats.at[0, 3])
        norm_back(turn + 1, layer, 0, normed_copy, inverse_copy, layer == 0)
        if layer == 1:
            gather(turn + 2)
            summing.advance()

    other = at((1 - chip) * block, block, block)
    mine = at(chip * block, block, block)
    b.rows_send[...] = b.state[other, :].astype(BF)
    rows_copy = remote(b.rows_send, b.rows_recv, 16, {"tensor": flip(tensor, 2)})
    rows_copy.start()
    sections = r.ada_scale.shape[0]
    for k in range(2):
        b.small_buf[0, 0, k : k + 1, :] = vec[2 * k : 2 * k + 1, :]
        b.small_buf[0, 0, 2 + k : 3 + k, :] = vec[2 * k + 1 : 2 * k + 2, :]
        for index in range(sections):
            chosen = jnp.where(section == index, 1.0, 0.0).astype(F32)
            for which in range(2):
                row = 4 + 2 * sections * which + 2 * index + k
                source = 4 + 2 * k + which
                b.small_buf[0, 0, row : row + 1, :] = vec[source : source + 1, :] * chosen

    def small_copy(i):
        return pltpu.make_async_remote_copy(
            src_ref=b.small_buf.at[0, i],
            dst_ref=b.small_buf.at[1, i],
            send_sem=b.small_send.at[i],
            recv_sem=b.small_recv.at[i],
            device_id=partners[i],
            device_id_type=MESH,
        )

    small_copy(0).start()
    for i in range(len(partners)):
        summing.advance()
        small_copy(i).wait()
        total = b.small_buf[0, i] + b.small_buf[1, i]
        if i + 1 < len(partners):
            b.small_buf[0, i + 1] = total
            small_copy(i + 1).start()
        else:
            o.gain_out[...] = total[0:2]
            o.bias_out[...] = total[2:4]
            for index in range(sections):
                row = 4 + 2 * index
                o.scale_out[index] = total[row : row + 2]
                row += 2 * sections
                o.shift_out[index] = total[row : row + 2]
    rows_copy.wait()
    hidden_copy.wait()
    hidden_own_copy.wait()
    o.frames_grad[chip] = b.state[mine, :]
    o.frames_grad[1 - chip] = b.rows_recv[...].astype(F32)
    summing.drain()


ROWS, DOWN, SLOPE, ACT, UP, QKVA, WATTN, PACK = range(8)


class BackIn(NamedTuple):
    hidden: Any
    grad_in: Any
    mats: Any
    norms: Any
    inverses: Any
    foreign_weights: Any
    w_attn: Any
    w_up: Any
    w_down: Any
    lengths: Any
    codebook: Any
    ln_gain: Any
    ada_scale: Any
    lse: Any


class BackOut(NamedTuple):
    down: Any
    up: Any
    attn: Any
    own: Any
    foreign: Any
    hidden_out: Any
    frames_grad: Any
    gain_out: Any
    bias_out: Any
    scale_out: Any
    shift_out: Any


class BackScratch(NamedTuple):
    gains: Any
    bias: Any
    slots: Any
    dpre: Any
    full: Any
    rs_send: Any
    rs_recv: Any
    state: Any
    keep: Any
    normed: Any
    inverse: Any
    stage: Any
    dk: Any
    dv: Any
    grad_att: Any
    vec: Any
    rows_send: Any
    rows_recv: Any
    small_buf: Any
    acc: Any
    seg: Any
    own_view: Any
    slot_sem: Any
    misc_sem: Any
    stage_sem: Any
    ex_send: Any
    ex_recv: Any
    small_send: Any
    small_recv: Any
    send_sem: Any
    recv_sem: Any
    copy_sem: Any
    view_sem: Any


def backward(inputs, size):
    half, width = inputs.grad_in.shape
    length = 2 * half
    block = length // 4
    bits = dp_bits(size)
    rows = 256
    matrices = 6
    chunks = matrices * length // rows
    stages = 2 * len(bits) + 1
    ring = min(chunks, max(2 * Summing.AHEAD + len(bits), 2 * len(bits)) + 1)
    steps = halvings(bits, rows, width)
    sections = inputs.ada_scale.shape[0]
    small_rows = 4 + 4 * sections
    exchanges = len(bits) + 2
    whole = jax.ShapeDtypeStruct((chunks, rows, width), BF)
    dma = pltpu.SemaphoreType.DMA
    shapes = BackScratch(
        gains=pltpu.VMEM((4, width), F32),
        bias=pltpu.VMEM((length, 1), F32),
        slots=pltpu.VMEM((5, length, width), BF),
        dpre=pltpu.VMEM((2, length, width), BF),
        full=pltpu.VMEM((2, length, width), BF),
        rs_send=pltpu.VMEM((half, width), BF),
        rs_recv=pltpu.VMEM((2, half, width), BF),
        state=pltpu.VMEM((half, width), F32),
        keep=pltpu.VMEM((half, width), F32),
        normed=pltpu.VMEM((half, width), F32),
        inverse=pltpu.VMEM((half, LANES), F32),
        stage=pltpu.VMEM((length // rows, rows, width), BF),
        dk=pltpu.VMEM((length, LANES), F32),
        dv=pltpu.VMEM((length, LANES), F32),
        grad_att=pltpu.VMEM((length, width // 4), BF),
        vec=pltpu.VMEM((8, width), F32),
        rows_send=pltpu.VMEM((block, width), BF),
        rows_recv=pltpu.VMEM((block, width), BF),
        small_buf=pltpu.VMEM((2, exchanges, small_rows, width), F32),
        acc=pltpu.VMEM((ring, rows, width), BF),
        seg=pltpu.VMEM((chunks,) + steps[-1][:2], BF),
        own_view=pltpu.VMEM((2, rows, width), BF),
        slot_sem=dma((5,)),
        misc_sem=dma((4,)),
        stage_sem=dma((1,)),
        ex_send=dma((18,)),
        ex_recv=dma((18,)),
        small_send=dma((exchanges,)),
        small_recv=dma((exchanges,)),
        send_sem=dma((stages, chunks)),
        recv_sem=dma((stages, chunks)),
        copy_sem=dma((chunks,)),
        view_sem=dma((2,)),
    )
    scratch = list(shapes)
    scratch += [pltpu.VMEM((ring,) + step[:2], BF) for step in steps]
    any_spec = pl.BlockSpec(memory_space=pl.ANY)
    vmem_spec = pl.BlockSpec(memory_space=pltpu.VMEM)
    smem_spec = pl.BlockSpec(memory_space=pltpu.SMEM)
    outs = pl.pallas_call(
        functools.partial(back_kernel, bits),
        in_specs=[any_spec] * 9 + [smem_spec] * 2 + [vmem_spec] * 3,
        out_specs=[any_spec] * 6 + [vmem_spec] * 5,
        out_shape=[jax.ShapeDtypeStruct((2, length // rows, rows, width), BF)] * 3
        + [whole] * 2
        + [
            jax.ShapeDtypeStruct((2, block, width), BF),
            jax.ShapeDtypeStruct((2, block, width), F32),
            jax.ShapeDtypeStruct((2, width), F32),
            jax.ShapeDtypeStruct((2, width), F32),
            jax.ShapeDtypeStruct((sections, 2, width), F32),
            jax.ShapeDtypeStruct((sections, 2, width), F32),
        ],
        scratch_shapes=scratch,
        compiler_params=pltpu.CompilerParams(
            vmem_limit_bytes=VMEM_BYTES, collective_id=1, has_side_effects=True
        ),
        name="backward",
    )(*inputs)
    return BackOut(*outs)


def choose_maps(target, shared, adaptive, section):
    target[0:2, :] = shared[...]
    chosen = jnp.zeros_like(shared[...])
    for index in range(adaptive.shape[0]):
        chosen = jnp.where(section == index, adaptive[index], chosen)
    target[2:4, :] = chosen


class Fetching:
    SKEW = 2
    STAGES = 3

    def __init__(self, sources, targets, send_sem, recv_sem):
        self.sources, self.targets = sources, targets
        self.send_sem, self.recv_sem = send_sem, recv_sem
        self.dp = lax.axis_index("dp")
        self.tensor = lax.axis_index("tensor")
        self.unit = sources[0].shape[0] // 16
        self.items = 2 * len(sources)
        self.step = 0

    def remote(self, stage, item, sub, rows, device):
        target = self.targets[item // 2].at[rows]
        return pltpu.make_async_remote_copy(
            src_ref=self.sources[item // 2].at[rows] if stage == 0 else target,
            dst_ref=target,
            send_sem=self.send_sem.at[stage, item, sub],
            recv_sem=self.recv_sem.at[stage, item, sub],
            device_id=device,
            device_id_type=MESH,
        )

    def copies(self, stage, item):
        pieces = []
        for sub in range(2):
            first_bit = 1 + sub
            low = lax.rem(self.dp // first_bit, 2)
            high = lax.rem(self.dp // (3 - first_bit), 2)
            base = (8 * (item % 2) + 4 * sub) * self.unit
            quarter = self.unit
            if stage < 2:
                rows = at(base + (2 * high + low) * quarter, quarter, 16)
            else:
                rows = at(base + high * 2 * quarter, 2 * quarter, 16)
            if stage == 0:
                device = {"tensor": flip(self.tensor, 2)}
            else:
                device = {"dp": flip(self.dp, first_bit if stage == 1 else 3 - first_bit)}
            pieces.append(self.remote(stage, item, sub, rows, device))
        return pieces

    def advance(self):
        step = self.step
        for stage in range(self.STAGES, 0, -1):
            item = step - self.SKEW * stage
            if 0 <= item < self.items:
                for copy in self.copies(stage - 1, item):
                    copy.wait_recv()
                if stage < self.STAGES:
                    for copy in self.copies(stage, item):
                        copy.start()
        if step < self.items:
            for copy in self.copies(0, step):
                copy.start()
        self.step += 1

    def need(self, matrix):
        while self.step <= 2 * matrix + 1 + self.SKEW * self.STAGES:
            self.advance()

    def drain(self):
        self.need(len(self.sources) - 1)
        for item in range(self.items):
            for stage in range(self.STAGES):
                for copy in self.copies(stage, item):
                    copy.wait_send()


def forward_kernel(bits, *refs):
    r, refs = ForwardIn(*refs[: len(ForwardIn._fields)]), refs[len(ForwardIn._fields) :]
    o, refs = ForwardOut(*refs[: len(ForwardOut._fields)]), refs[len(ForwardOut._fields) :]
    b = ForwardScratch(*refs)
    dp = lax.axis_index("dp")
    tensor = lax.axis_index("tensor")
    chip = tensor // 2
    core = lax.rem(tensor, 2)
    half, width = b.state.shape
    length = 2 * half
    block = length // 4
    part_cols = width // 4
    core_partner = {"tensor": flip(tensor, 1)}
    chip_partner = {"tensor": flip(tensor, 2)}
    partners = [core_partner, chip_partner] + [{"dp": flip(dp, bit)} for bit in bits[:2]]

    barrier = pltpu.get_barrier_semaphore()
    for partner in partners:
        pl.semaphore_signal(barrier, inc=1, device_id=partner, device_id_type=MESH)
    pl.semaphore_wait(barrier, len(partners))

    def remote(source, target, sem, device):
        return pltpu.make_async_remote_copy(
            src_ref=source,
            dst_ref=target,
            send_sem=b.ex_send.at[sem],
            recv_sem=b.ex_recv.at[sem],
            device_id=device,
            device_id_type=MESH,
        )

    def local(source, target, sem):
        return pltpu.make_async_copy(source, target, b.local_sem.at[sem])

    frames_copy = remote(r.frames.at[1 - chip], b.frames_got, 17, chip_partner)
    frames_copy.start()
    own_copy = local(r.frames.at[chip], b.frames_own, 0)
    own_copy.start()

    slots = Slots(b.slots, b.slot_sem)

    def pack_copies(layer, slot):
        pairs = []
        for i in range(3):
            pairs.append((r.w_qkv.at[layer, i], slot.at[:, pl.ds(i * part_cols, part_cols)]))
        for k in range(4):
            span = pl.ds(k * part_cols, part_cols)
            pairs.append((r.w_out.at[layer, :, span], slot.at[span, pl.ds(3 * part_cols, part_cols)]))
        return [
            pltpu.make_async_copy(source, target, b.pack_sem.at[layer, i])
            for i, (source, target) in enumerate(pairs)
        ]

    choose_maps(b.gains, r.ln_gain, r.ada_scale, r.codebook[chip])
    choose_maps(b.shifts, r.ln_bias, r.ada_shift, r.codebook[chip])
    key_at = lax.broadcasted_iota(jnp.int32, (1, length), 1)
    b.bias[...] = jnp.where(key_at < r.lengths[chip], 0.0, -1e30).astype(F32)
    pack_slots = [slots.reserve((WATTN, 0)), slots.reserve(PACK)]
    packs = [pack_copies(layer, slot) for layer, slot in enumerate(pack_slots)]
    stores = [
        pltpu.make_async_copy(slot, o.w_attn.at[layer], b.pack_sem.at[layer, 7])
        for layer, slot in enumerate(pack_slots)
    ]
    for pack in packs:
        for copy in pack:
            copy.start()
    for copy in packs[0]:
        copy.wait()
    stores[0].start()
    stores[0].wait()
    sources, targets = [], []
    for layer in range(2):
        sources += [o.w_attn.at[layer], r.w_up.at[layer], r.w_down.at[layer]]
        targets += [o.foreign_weights.at[layer, i] for i in range(3)]
    fetching = Fetching(sources, targets, b.send_sem, b.recv_sem)
    fetching.advance()
    for copy in packs[1]:
        copy.wait()
    stores[1].start()
    own_copy.wait()
    frames_copy.wait()
    fetching.advance()
    fetching.advance()
    b.state[at(chip * block, block, block), :] = b.frames_own[...].astype(F32)
    b.state[at((1 - chip) * block, block, block), :] = b.frames_got[...].astype(F32)
    grad_copy = remote(r.out_grad.at[1 - chip], b.grad_got, 16, chip_partner)
    grad_own_copy = local(r.out_grad.at[chip], b.grad_own, 0)

    def exchange_copies(turn):
        full = b.full.at[turn % 2]
        spans = [at((2 * j + core) * block, block, block) for j in range(2)]
        return [remote(full.at[s], full.at[s], 4 * turn + j, core_partner) for j, s in enumerate(spans)]

    def scatter(turn, partial):
        copies = [
            remote(
                b.rs_send.at[pl.ds(j * block, block)],
                b.rs_recv.at[turn % 2, pl.ds(j * block, block)],
                4 * turn + 2 + j,
                core_partner,
            )
            for j in range(2)
        ]
        for j in range(2):
            span = at((2 * j + 1 - core) * block, block, block)
            b.rs_send[pl.ds(j * block, block), :] = partial(span).astype(BF)
            copies[j].start()
        for j in range(2):
            span = at((2 * j + core) * block, block, block)
            b.keep[pl.ds(j * block, block), :] = partial(span)
        for copy in copies:
            copy.wait()

    saves = []

    def save(source, target, sem):
        copy = local(source, target, sem)
        copy.start()
        saves.append(copy)

    def settle():
        for copy in saves:
            copy.wait()
        saves.clear()

    norm_copies = []

    def norm(turn, layer, which, add):
        for copy in norm_copies:
            copy.wait()
        norm_copies.clear()
        gain = b.gains[2 * layer + which : 2 * layer + which + 1, :]
        shift = b.shifts[2 * layer + which : 2 * layer + which + 1, :]
        step = 128
        copies = exchange_copies(turn)
        for j in range(2):

            def rows_body(i, _, j=j):
                span = at(j * block + i * step, step, step)
                state = b.state[span, :]
                if add:
                    state = state + (b.keep[span, :] + b.rs_recv[(turn - 1) % 2, span, :].astype(F32))
                    b.state[span, :] = state
                centred = state - jnp.mean(state, axis=-1, keepdims=True)
                variance = jnp.mean(centred * centred, axis=-1, keepdims=True)
                inverse = lax.rsqrt(variance + 1e-05)
                normed = centred * inverse
                b.normed[span, :] = normed
                b.inverse[span, :] = jnp.broadcast_to(inverse, (step, LANES))
                b.full[turn % 2, at((2 * j + core) * block + i * step, step, step), :] = (
                    normed * gain + shift
                ).astype(BF)
                return 0

            lax.fori_loop(0, block // step, rows_body, 0)
            copies[j].start()
        norm_copies.append(local(b.normed, o.norms.at[layer, which], 1))
        norm_copies.append(local(b.inverse, o.inverses.at[layer, which], 2))
        for copy in norm_copies:
            copy.start()

        def arrive(copies=copies):
            for copy in copies:
                copy.wait()
            save(b.full.at[turn % 2], o.mats.at[layer, 3 * which], 3)

        return arrive

    for layer in range(2):
        turn = 2 * layer
        arrive = norm(turn, layer, 0, layer == 1)
        if layer == 0:
            stores[1].wait()
            fetching.advance()
        full = b.full.at[turn % 2]
        settle()
        fetching.advance()
        for part in range(2):
            if part == 1:
                fetching.need(3 * layer)
                slots.load((WATTN, 1), o.foreign_weights.at[layer, 0])
            quiet = [] if layer == 0 and part == 0 else [None]

            def steps(quiet=quiet):
                if quiet:
                    quiet.pop()
                else:
                    fetching.advance()

            attend_part(
                layer == 0, full, slots.get((WATTN, part)), b.bias, b.acts.at[part], o.lse.at[layer, part],
                arrive if part == 0 else lambda: None, steps,
            )
            save(b.acts.at[part], o.mats.at[layer, 1 + part], 4 + part)
            if part == 0:
                slots.load((UP, 0), r.w_up.at[layer])
                slots.load((DOWN, 0), r.w_down.at[layer])
        weights = [slots.get((WATTN, part)) for part in range(2)]

        def out_partial(span, weights=weights):
            cols = slice(3 * part_cols, None)
            first, second = b.acts[0, span, cols], b.acts[1, span, cols]
            spans = [pl.ds(k * part_cols, part_cols) for k in range(4)]
            return jnp.concatenate(
                [mm(first, weights[0][s, cols]) + mm(second, weights[1][s, cols]) for s in spans], axis=1
            )

        scatter(turn, out_partial)
        slots.drop((WATTN, 0), (WATTN, 1))
        fetching.advance()
        turn += 1
        if layer == 1:
            grad_copy.start()
            grad_own_copy.start()
        arrive = norm(turn, layer, 1, True)
        full = b.full.at[turn % 2]
        settle()
        fetching.advance()
        for part in range(2):
            if part == 1:
                fetching.need(3 * layer + 1)
                slots.load((UP, 1), o.foreign_weights.at[layer, 1])
            up = slots.get((UP, part))

            def up_body(i, part=part, up=up, full=full):
                rows = at(i * block, block, block)
                for first in range(0, width, 256):
                    cols = pl.ds(first, 256)
                    active, slope = gelu_parts(mm(full[rows, :], up[:, cols]))
                    b.acts[part, rows, cols] = active.astype(BF)
                    b.slope[part, rows, cols] = slope.astype(BF)

            own_rows_first(up_body, arrive if part == 0 else lambda: None)
            save(b.acts.at[part], o.mats.at[layer, 4 + part], 4 + part)
            save(b.slope.at[part], o.mats.at[layer, 6 + part], 6 + part)
            slots.drop((UP, part))
            if layer == 1 and part == 0:
                fetching.advance()
        fetching.need(3 * layer + 2)
        slots.load((DOWN, 1), o.foreign_weights.at[layer, 2])
        downs = [slots.get((DOWN, part)) for part in range(2)]

        def down_partial(span, downs=downs):
            return mm(b.acts[0, span, :], downs[0][...]) + mm(b.acts[1, span, :], downs[1][...])

        scatter(turn, down_partial)
        slots.drop((DOWN, 0), (DOWN, 1))
        if layer == 0:
            slots.rename(PACK, (WATTN, 0))

    for j in range(2):
        span = pl.ds(j * block, block)
        total = b.state[span, :] + (b.keep[span, :] + b.rs_recv[1, span, :].astype(F32))
        o.hidden[j] = total.astype(BF)
    grad_own_copy.wait()
    grad_copy.wait()
    o.grad_in[at(chip * block, block, block), :] = b.grad_own[...].astype(F32)
    o.grad_in[at((1 - chip) * block, block, block), :] = b.grad_got[...].astype(F32)
    fetching.drain()
    settle()
    for copy in norm_copies:
        copy.wait()


class ForwardIn(NamedTuple):
    frames: Any
    out_grad: Any
    w_qkv: Any
    w_out: Any
    w_up: Any
    w_down: Any
    lengths: Any
    codebook: Any
    ln_gain: Any
    ln_bias: Any
    ada_scale: Any
    ada_shift: Any


class ForwardOut(NamedTuple):
    mats: Any
    norms: Any
    inverses: Any
    foreign_weights: Any
    w_attn: Any
    lse: Any
    grad_in: Any
    hidden: Any


class ForwardScratch(NamedTuple):
    gains: Any
    shifts: Any
    bias: Any
    slots: Any
    acts: Any
    slope: Any
    full: Any
    rs_send: Any
    rs_recv: Any
    state: Any
    keep: Any
    normed: Any
    inverse: Any
    frames_own: Any
    frames_got: Any
    grad_own: Any
    grad_got: Any
    slot_sem: Any
    local_sem: Any
    pack_sem: Any
    ex_send: Any
    ex_recv: Any
    send_sem: Any
    recv_sem: Any


def forward(inputs, size):
    block, width = inputs.frames.shape[1:]
    half, length = 2 * block, 4 * block
    bits = dp_bits(size)
    dma = pltpu.SemaphoreType.DMA
    rows = pltpu.VMEM((block, width), BF)
    scratch = ForwardScratch(
        gains=pltpu.VMEM((4, width), F32),
        shifts=pltpu.VMEM((4, width), F32),
        bias=pltpu.VMEM((1, length), F32),
        slots=pltpu.VMEM((5, length, width), BF),
        acts=pltpu.VMEM((2, length, width), BF),
        slope=pltpu.VMEM((2, length, width), BF),
        full=pltpu.VMEM((2, length, width), BF),
        rs_send=pltpu.VMEM((half, width), BF),
        rs_recv=pltpu.VMEM((2, half, width), BF),
        state=pltpu.VMEM((half, width), F32),
        keep=pltpu.VMEM((half, width), F32),
        normed=pltpu.VMEM((half, width), F32),
        inverse=pltpu.VMEM((half, LANES), F32),
        frames_own=rows,
        frames_got=rows,
        grad_own=rows,
        grad_got=rows,
        slot_sem=dma((5,)),
        local_sem=dma((8,)),
        pack_sem=dma((2, 8)),
        ex_send=dma((18,)),
        ex_recv=dma((18,)),
        send_sem=dma((3, 12, 2)),
        recv_sem=dma((3, 12, 2)),
    )
    out_shape = ForwardOut(
        mats=jax.ShapeDtypeStruct((2, 8, length, width), BF),
        norms=jax.ShapeDtypeStruct((2, 2, half, width), F32),
        inverses=jax.ShapeDtypeStruct((2, 2, half, LANES), F32),
        foreign_weights=jax.ShapeDtypeStruct((2, 3, length, width), BF),
        w_attn=jax.ShapeDtypeStruct((2, length, width), BF),
        lse=jax.ShapeDtypeStruct((2, 2, width // (4 * LANES), 8, length), F32),
        grad_in=jax.ShapeDtypeStruct((half, width), F32),
        hidden=jax.ShapeDtypeStruct((2, block, width), BF),
    )
    any_spec = pl.BlockSpec(memory_space=pl.ANY)
    vmem_spec = pl.BlockSpec(memory_space=pltpu.VMEM)
    smem_spec = pl.BlockSpec(memory_space=pltpu.SMEM)
    outs = pl.pallas_call(
        functools.partial(forward_kernel, bits),
        in_specs=[any_spec] * 6 + [smem_spec] * 2 + [vmem_spec] * 4,
        out_specs=[any_spec] * 5 + [vmem_spec] * 3,
        out_shape=list(out_shape),
        scratch_shapes=list(scratch),
        compiler_params=pltpu.CompilerParams(
            vmem_limit_bytes=VMEM_BYTES, collective_id=2, has_side_effects=True
        ),
        name="forward",
    )(*inputs)
    return ForwardOut(*outs)


def per_device(
    frames, lengths, codebook, ln_gain, ln_bias, ada_scale, ada_shift, w_qkv, w_out, w_up, w_down, out_grad
):
    size = lax.axis_size("dp")
    ahead = forward(
        ForwardIn(
            frames,
            out_grad,
            w_qkv.transpose(0, 2, 1, 3),
            w_out,
            w_up,
            w_down,
            lengths,
            codebook,
            ln_gain,
            ln_bias,
            ada_scale,
            ada_shift,
        ),
        size,
    )
    back = backward(
        BackIn(
            ahead.hidden,
            ahead.grad_in,
            ahead.mats,
            ahead.norms,
            ahead.inverses,
            ahead.foreign_weights,
            ahead.w_attn,
            w_up,
            w_down,
            lengths,
            codebook,
            ln_gain,
            ada_scale,
            ahead.lse,
        ),
        size,
    )
    layers, part, width = w_out.shape
    attn = back.attn.reshape(layers, width, width)
    grad_qkv = jnp.stack([attn[:, :, i * part : (i + 1) * part].astype(F32) for i in range(3)], axis=1)
    quarters = [back.attn[:, k, :, 3 * part :].astype(F32) for k in range(width // part)]
    grad_out = jnp.concatenate(quarters, axis=2)
    return (
        back.hidden_out,
        back.frames_grad,
        back.gain_out,
        back.bias_out,
        back.scale_out,
        back.shift_out,
        grad_qkv.transpose(0, 2, 1, 3),
        grad_out.reshape(w_out.shape),
        back.up.astype(F32).reshape(w_up.shape),
        back.down.astype(F32).reshape(w_down.shape),
    )


def solution(mesh):
    placed = (
        P("dp", "tensor", None),
        P("dp"),
        P("dp"),
        P(),
        P(),
        P(),
        P(),
        P(None, None, None, "tensor"),
        P(None, "tensor", None),
        P(None, None, "tensor"),
        P(None, "tensor", None),
        P("dp", "tensor", None),
    )
    return jax.shard_map(
        per_device,
        mesh=mesh,
        in_specs=placed,
        out_specs=(
            P("dp", "tensor", None),
            P("dp", "tensor", None),
            P(),
            P(),
            P(),
            P(),
            P(None, None, None, "tensor"),
            P(None, "tensor", None),
            P(None, None, "tensor"),
            P(None, "tensor", None),
        ),
        check_vma=False,
    )
```
